32 devices in a mesh: dp: 4 (over x, core), chan: 8 (over z, y).
Axes of the slice: x: 2, y: 2, z: 4, core: 2. Of those that a mesh axis runs over, the one named last changes fastest.
Arguments:
- crop_maps: float32 [8, 128, 3136], P('dp', 'chan'), may hold values from -12 to 12
- out_cotangent: float32 [8, 256, 3136], P('dp', 'chan'), may hold values from -12 to 12
- norm_group: int32 [8], replicated, may hold values from 0 to 3, as said below
- scale_class: int32 [8], replicated, may hold values from 0 to 1
- entry_conv: float32 [256, 9, 128], P('chan'), may hold values from -0.1875 to 0.1875
- middle_conv: float32 [256, 9, 256], P('chan'), may hold values from -0.125 to 0.125
- shortcut_map: float32 [256, 128], P('chan'), may hold values from -0.5 to 0.5
- decoder_conv: float32 [256, 9, 256], P('chan'), may hold values from -0.125 to 0.125
- style_map: float32 [256, 256], P('chan'), may hold values from -3 to 3
- narrow_gain_table: float32 [4, 128], P(None, 'chan'), may hold values from -1 to 1.3
- wide_gain_table: float32 [5, 256], P(None, 'chan'), may hold values from -1 to 1.3
- entry_moment: float32 [256, 9, 128], P('chan'), may hold values from -0.0012207031 to 0.0012207031
- middle_moment: float32 [256, 9, 256], P('chan'), may hold values from -0.0012207031 to 0.0012207031
- shortcut_moment: float32 [256, 128], P('chan'), may hold values from -0.0012207031 to 0.0012207031
- decoder_moment: float32 [256, 9, 256], P('chan'), may hold values from -0.0012207031 to 0.0012207031
- style_moment: float32 [256, 256], P('chan'), may hold values from -0.0012207031 to 0.0012207031
- narrow_moment: float32 [4, 128], P(None, 'chan'), may hold values from -0.0012207031 to 0.0012207031
- wide_moment: float32 [5, 256], P(None, 'chan'), may hold values from -0.0012207031 to 0.0012207031
- entry_square: float32 [256, 9, 128], P('chan'), may hold values from 6.3505934e-10 to 2.5402374e-09
- middle_square: float32 [256, 9, 256], P('chan'), may hold values from 6.3505934e-10 to 2.5402374e-09
- shortcut_square: float32 [256, 128], P('chan'), may hold values from 6.3505934e-10 to 2.5402374e-09
- decoder_square: float32 [256, 9, 256], P('chan'), may hold values from 6.3505934e-10 to 2.5402374e-09
- style_square: float32 [256, 256], P('chan'), may hold values from 6.3505934e-10 to 2.5402374e-09
- narrow_square: float32 [4, 128], P(None, 'chan'), may hold values from 6.3505934e-10 to 2.5402374e-09
- wide_square: float32 [5, 256], P(None, 'chan'), may hold values from 6.3505934e-10 to 2.5402374e-09
Outputs:
- block_out: float32 [8, 256, 3136], P('dp', 'chan')
- input_grad: float32 [8, 128, 3136], P('dp', 'chan')
- entry_weight: float32 [256, 9, 128], P('chan')
- entry_first: float32 [256, 9, 128], P('chan')
- entry_second: float32 [256, 9, 128], P('chan')
- middle_weight: float32 [256, 9, 256], P('chan')
- middle_first: float32 [256, 9, 256], P('chan')
- middle_second: float32 [256, 9, 256], P('chan')
- shortcut_weight: float32 [256, 128], P('chan')
- shortcut_first: float32 [256, 128], P('chan')
- shortcut_second: float32 [256, 128], P('chan')
- decoder_weight: float32 [256, 9, 256], P('chan')
- decoder_first: float32 [256, 9, 256], P('chan')
- decoder_second: float32 [256, 9, 256], P('chan')
- style_weight: float32 [256, 256], P('chan')
- style_first: float32 [256, 256], P('chan')
- style_second: float32 [256, 256], P('chan')
- narrow_weight: float32 [4, 128], P(None, 'chan')
- narrow_first: float32 [4, 128], P(None, 'chan')
- narrow_second: float32 [4, 128], P(None, 'chan')
- wide_weight: float32 [5, 256], P(None, 'chan')
- wide_first: float32 [5, 256], P(None, 'chan')
- wide_second: float32 [5, 256], P(None, 'chan')
- grad_norm: float32 [], replicated
The draws below stay inside these ranges and needn't reach their ends.
Inputs may be any that keep to these rules, and one draw needn't show every extreme that they name: `norm_group`: each of the 4 groups holds exactly 2 crops.
All inputs are finite; a program needn't handle non-finite values.
Results may differ from the reference program's by a relative error of at most 0.0003.
Values sent between devices are 32-bit elements; how exact they have to be, the bound alone decides.
No kernel may reach another device: no remote copies, remote signals or barrier semaphores. Data moves between devices by JAX's collectives and lax.ppermute only.
A program may use at most 192 MiB of HBM per device.

```python
import math
import jax
import jax.numpy as jnp
from jax import lax

CI = 128
CO = 256
H_BIG = 56
H_SMALL = 40
PIX = 3136
CROPS = 8
NGRP = 4
STEP = 10
NPARAM = 1574656


def draw_crop_maps(key, part):
    key = jax.random.fold_in(key, 3)
    values = jnp.clip(jax.random.normal(key, (CROPS, CI, PIX), jnp.float32), -4.0, 4.0)
    growth = 1.0 + 2.0 * jnp.arange(CROPS, dtype=jnp.float32) / max(CROPS - 1, 1)
    return values * growth[:, None, None]


def draw_out_cotangent(key, part):
    key = jax.random.fold_in(key, 5)
    values = jnp.clip(jax.random.normal(key, (CROPS, CO, PIX), jnp.float32), -4.0, 4.0)
    growth = 1.0 + 2.0 * jnp.arange(CO, dtype=jnp.float32) / max(CO - 1, 1)
    return values * growth[None, :, None]


def draw_norm_group(key, part):
    key = jax.random.fold_in(key, 7)
    labels = jnp.arange(CROPS, dtype=jnp.int32) % NGRP
    return jax.random.permutation(key, labels).astype(jnp.int32)


def gain_table(key, row_count, columns):
    gain_key = jax.random.fold_in(key, 11)
    shift_key = jax.random.fold_in(key, 23)
    gain_draw = jax.random.uniform(gain_key, (row_count, columns), jnp.float32, 0.7, 1.3)
    shifts = 0.3 * jnp.clip(jax.random.normal(shift_key, (row_count, columns), jnp.float32), -3.0, 3.0)
    row_ids = jnp.arange(row_count)
    is_gain = (row_ids % 2 == 0) & (row_ids < 4)
    return jnp.where(is_gain[:, None], gain_draw, shifts)


def draw_narrow_gain_table(key, part):
    key = jax.random.fold_in(key, 13)
    return gain_table(key, 4, CI)


def draw_wide_gain_table(key, part):
    key = jax.random.fold_in(key, 17)
    return gain_table(key, 5, CO)


def plant(values, key, least, largest):
    index_at = [jax.random.randint(jax.random.fold_in(key, axis), (), 0, length) for axis, length in enumerate(values.shape)]
    main_axis = values.shape.index(max(values.shape))
    next_to = index_at[:main_axis] + [(index_at[main_axis] + 1) % values.shape[main_axis]] + index_at[main_axis + 1:]
    return values.at[tuple(index_at)].set(least).at[tuple(next_to)].set(largest)


def block_scale(own_key, dims, split, smallest, largest):
    gain, own = 1.0, jax.random.fold_in(own_key, 6)
    for dim, parts in split:
        draws = jnp.exp(jax.random.uniform(jax.random.fold_in(own, dim), (parts,), jnp.float32, smallest / len(split), largest / len(split)))
        gain = gain * jnp.repeat(draws, dims[dim] // parts).reshape([-1 if axis == dim else 1 for axis in range(len(dims))])
    return gain


def normal_values(key, extent, spread, limit, shards=(), kind=jnp.bfloat16):
    loudness = block_scale(key, extent, shards, -0.22, 0.18) if shards else 1.0
    values = jax.random.normal(key, extent, jnp.float32) * spread * loudness
    return jnp.minimum(jnp.maximum(values, -limit), limit).astype(kind)


def setup_inputs(seed: int = 0) -> dict:
    key_list = jax.random.split(jax.random.key(seed), 26)
    return {
        "crop_maps": draw_crop_maps(jax.random.fold_in(key_list[25], 71), 0),
        "out_cotangent": draw_out_cotangent(jax.random.fold_in(key_list[25], 71), 0),
        "norm_group": draw_norm_group(jax.random.fold_in(key_list[25], 71), 0),
        "scale_class": plant(jax.random.randint(key_list[3], (CROPS,), 0, 2), jax.random.fold_in(key_list[3], 1), 0, 1).astype(jnp.int32),
        "entry_conv": normal_values(key_list[4], (CO, 9, CI), (9 * CI) ** -0.5, 0.1875, ((0, 8),), jnp.float32),
        "middle_conv": normal_values(key_list[5], (CO, 9, CO), (9 * CO) ** -0.5, 0.125, ((0, 8),), jnp.float32),
        "shortcut_map": normal_values(key_list[6], (CO, CI), CI ** -0.5, 0.5, ((0, 8),), jnp.float32),
        "decoder_conv": normal_values(key_list[7], (CO, 9, CO), (9 * CO) ** -0.5, 0.125, ((0, 8),), jnp.float32),
        "style_map": normal_values(key_list[8], (CO, CO), 4 ** -0.5, 3.0, ((0, 8),), jnp.float32),
        "narrow_gain_table": draw_narrow_gain_table(jax.random.fold_in(key_list[25], 71), 0),
        "wide_gain_table": draw_wide_gain_table(jax.random.fold_in(key_list[25], 71), 0),
        "entry_moment": normal_values(key_list[11], (CO, 9, CI), (0.111 / NPARAM ** 0.5), 0.0012207031, ((0, 8),), jnp.float32),
        "middle_moment": normal_values(key_list[12], (CO, 9, CO), (0.111 / NPARAM ** 0.5), 0.0012207031, ((0, 8),), jnp.float32),
        "shortcut_moment": normal_values(key_list[13], (CO, CI), (0.111 / NPARAM ** 0.5), 0.0012207031, ((0, 8),), jnp.float32),
        "decoder_moment": normal_values(key_list[14], (CO, 9, CO), (0.111 / NPARAM ** 0.5), 0.0012207031, ((0, 8),), jnp.float32),
        "style_moment": normal_values(key_list[15], (CO, CO), (0.111 / NPARAM ** 0.5), 0.0012207031, ((0, 8),), jnp.float32),
        "narrow_moment": normal_values(key_list[16], (4, CI), (0.111 / NPARAM ** 0.5), 0.0012207031, ((1, 8),), jnp.float32),
        "wide_moment": normal_values(key_list[17], (5, CO), (0.111 / NPARAM ** 0.5), 0.0012207031, ((1, 8),), jnp.float32),
        "entry_square": jnp.clip(jnp.exp(math.log(2.5402373537986023e-09) - 1.3862944 * jax.random.uniform(key_list[18], (CO, 9, CI), jnp.float32) ** block_scale(key_list[18], (CO, 9, CI), ((0, 8),), -0.2, 0.2)), 6.350593384496506e-10, 2.5402373537986023e-09),
        "middle_square": jnp.clip(jnp.exp(math.log(2.5402373537986023e-09) - 1.3862944 * jax.random.uniform(key_list[19], (CO, 9, CO), jnp.float32) ** block_scale(key_list[19], (CO, 9, CO), ((0, 8),), -0.2, 0.2)), 6.350593384496506e-10, 2.5402373537986023e-09),
        "shortcut_square": jnp.clip(jnp.exp(math.log(2.5402373537986023e-09) - 1.3862944 * jax.random.uniform(key_list[20], (CO, CI), jnp.float32) ** block_scale(key_list[20], (CO, CI), ((0, 8),), -0.2, 0.2)), 6.350593384496506e-10, 2.5402373537986023e-09),
        "decoder_square": jnp.clip(jnp.exp(math.log(2.5402373537986023e-09) - 1.3862944 * jax.random.uniform(key_list[21], (CO, 9, CO), jnp.float32) ** block_scale(key_list[21], (CO, 9, CO), ((0, 8),), -0.2, 0.2)), 6.350593384496506e-10, 2.5402373537986023e-09),
        "style_square": jnp.clip(jnp.exp(math.log(2.5402373537986023e-09) - 1.3862944 * jax.random.uniform(key_list[22], (CO, CO), jnp.float32) ** block_scale(key_list[22], (CO, CO), ((0, 8),), -0.2, 0.2)), 6.350593384496506e-10, 2.5402373537986023e-09),
        "narrow_square": jnp.clip(jnp.exp(math.log(2.5402373537986023e-09) - 1.3862944 * jax.random.uniform(key_list[23], (4, CI), jnp.float32) ** block_scale(key_list[23], (4, CI), ((1, 8),), -0.2, 0.2)), 6.350593384496506e-10, 2.5402373537986023e-09),
        "wide_square": jnp.clip(jnp.exp(math.log(2.5402373537986023e-09) - 1.3862944 * jax.random.uniform(key_list[24], (5, CO), jnp.float32) ** block_scale(key_list[24], (5, CO), ((1, 8),), -0.2, 0.2)), 6.350593384496506e-10, 2.5402373537986023e-09),
    }


@jax.custom_vjp
def low(v):
    return lax.optimization_barrier(v.astype(jnp.bfloat16)).astype(jnp.float32)

@jax.custom_vjp
def low_back(v):
    return v

def low_keep(v):
    return (low(v), None)

def low_pass(kept, grad):
    return (grad,)

def back_keep(v):
    return (v, None)

def back_low(kept, grad):
    return (low(grad),)
low.defvjp(low_keep, low_pass)
low_back.defvjp(back_keep, back_low)
beta_one = 0.9
beta_two = 0.999
adam_eps = 1e-08
decay_rate = 0.01
clip_bound = 1.0
norm_eps = 1e-05
style_eps = 1e-06
highest = lax.Precision.HIGHEST

def grouped_batch_normalizer(values, inner_region, group_membership, element_counts):
    totals = jnp.dot(group_membership.T, lax.optimization_barrier(jnp.sum(values * inner_region, axis=2)), precision=highest)
    average = totals / element_counts
    centered = (values - jnp.dot(group_membership, average, precision=highest)[:, :, None]) * inner_region
    variance = jnp.dot(group_membership.T, lax.optimization_barrier(jnp.sum(centered * centered, axis=2)), precision=highest) / element_counts
    scaled = lax.rsqrt(variance + norm_eps)
    return centered * jnp.dot(group_membership, scaled, precision=highest)[:, :, None]

def conv_ref(values, weight):
    kernel = jnp.transpose(weight.reshape(weight.shape[0], 3, 3, weight.shape[2]), (0, 3, 1, 2))
    canvas = values.reshape(values.shape[0], values.shape[1], H_BIG, H_BIG)
    result = lax.conv_general_dilated(canvas, kernel, (1, 1), ((1, 1), (1, 1)), dimension_numbers=('NCHW', 'OIHW', 'NCHW'), precision=highest)
    return result.reshape(values.shape[0], weight.shape[0], H_BIG * H_BIG)

def adamw(weight, gradient, moment, square, rate, decay):
    first_new = beta_one * moment + (1.0 - beta_one) * gradient
    second_new = beta_two * square + (1.0 - beta_two) * gradient * gradient
    corrected_first = first_new / (1.0 - beta_one ** STEP)
    corrected_second = second_new / (1.0 - beta_two ** STEP)
    updated = weight - rate * (corrected_first / (jnp.sqrt(corrected_second) + adam_eps) + decay * weight)
    return (updated, first_new, second_new)

def reference(crop_maps, out_cotangent, norm_group, scale_class, entry_conv, middle_conv, shortcut_map, decoder_conv, style_map, narrow_gain_table, wide_gain_table, entry_moment, middle_moment, shortcut_moment, decoder_moment, style_moment, narrow_moment, wide_moment, entry_square, middle_square, shortcut_square, decoder_square, style_square, narrow_square, wide_square):
    group_membership = (norm_group[:, None] == jnp.arange(NGRP, dtype=jnp.int32)[None, :]).astype(jnp.float32)
    pixels = jnp.where(scale_class == 0, H_BIG * H_BIG, H_SMALL * H_SMALL).astype(jnp.float32)
    element_counts = jnp.dot(group_membership.T, pixels, precision=highest)[:, None]
    positions = jnp.arange(H_BIG * H_BIG, dtype=jnp.int32)
    small_area = ((positions // H_BIG < H_SMALL) & (positions % H_BIG < H_SMALL)).astype(jnp.float32)
    inner_region = jnp.where(scale_class[:, None] == 0, 1.0, small_area[None, :])[:, None, :]

    def forward(source, entry, middle, shortcut, decoder, style, narrow_channel_path, wide_channel_path):
        masked_feature_maps = source * inner_region
        standardized_entry = grouped_batch_normalizer(masked_feature_maps, inner_region, group_membership, element_counts)
        entry_input_map = jax.nn.silu(standardized_entry * narrow_channel_path[0][None, :, None] + narrow_channel_path[1][None, :, None]) * inner_region
        shortcut_input_map = (standardized_entry * narrow_channel_path[2][None, :, None] + narrow_channel_path[3][None, :, None]) * inner_region
        encoder_block_output = conv_ref(entry_input_map, entry)
        standardized_middle = grouped_batch_normalizer(encoder_block_output, inner_region, group_membership, element_counts)
        middle_input_map = jax.nn.silu(standardized_middle * wide_channel_path[0][None, :, None] + wide_channel_path[1][None, :, None]) * inner_region
        shortcut_out = jnp.einsum('oc,ncp->nop', shortcut, shortcut_input_map, precision=highest)
        hidden_activation = (shortcut_out + conv_ref(middle_input_map, middle)) * inner_region
        pooled = lax.optimization_barrier(jnp.sum(hidden_activation, axis=2)) / pixels[:, None]
        style_vec = pooled * lax.rsqrt(lax.optimization_barrier(jnp.sum(pooled * pooled, axis=1, keepdims=True)) + style_eps)
        style_contribution = jnp.dot(style_vec, style.T, precision=highest) + wide_channel_path[4][None, :]
        standardized_decoder = grouped_batch_normalizer(hidden_activation, inner_region, group_membership, element_counts)
        decoder_preactivation = standardized_decoder * wide_channel_path[2][None, :, None] + wide_channel_path[3][None, :, None] + style_contribution[:, :, None]
        decoder_in = jax.nn.silu(decoder_preactivation) * inner_region
        return (hidden_activation + conv_ref(decoder_in, decoder)) * inner_region
    block_out, pullback = jax.vjp(forward, crop_maps, entry_conv, middle_conv, shortcut_map, decoder_conv, style_map, narrow_gain_table, wide_gain_table)
    gradients = pullback(out_cotangent)
    params = (entry_conv, middle_conv, shortcut_map, decoder_conv, style_map, narrow_gain_table, wide_gain_table)
    moments = (entry_moment, middle_moment, shortcut_moment, decoder_moment, style_moment, narrow_moment, wide_moment)
    squares = (entry_square, middle_square, shortcut_square, decoder_square, style_square, narrow_square, wide_square)
    rates = (0.06, 0.04, 0.16, 0.04, 1.0, 0.4, 0.4)
    decays = (decay_rate, decay_rate, decay_rate, decay_rate, decay_rate, 0.0, 0.0)
    total_squares = jnp.zeros((), jnp.float32)
    for gradient in gradients[1:]:
        total_squares = total_squares + jnp.sum(gradient * gradient)
    grad_norm = jnp.sqrt(total_squares)
    clip_factor = jnp.minimum(1.0, clip_bound / grad_norm)
    results = [block_out, gradients[0]]
    for which in range(7):
        updated, first_new, second_new = adamw(params[which], gradients[which + 1] * clip_factor, moments[which], squares[which], rates[which], decays[which])
        results.append(updated)
        results.append(first_new)
        results.append(second_new)
    return (results[0], results[1], results[2], results[3], results[4], results[5], results[6], results[7], results[8], results[9], results[10], results[11], results[12], results[13], results[14], results[15], results[16], results[17], results[18], results[19], results[20], results[21], results[22], grad_norm)
```

```python
import functools

import jax
import jax.numpy as jnp
from jax import lax
from jax.experimental import pallas as pl
from jax.experimental.pallas import tpu as pltpu
from jax.sharding import PartitionSpec as P

SIDE = 56
H_SMALL = 40
NGRP = 4
STEP = 10
TAPS = 9

beta_one = 0.9
beta_two = 0.999
adam_eps = 1e-08
decay_rate = 0.01
clip_bound = 1.0
norm_eps = 1e-05
style_eps = 1e-06
highest = lax.Precision.HIGHEST
BOTH = ("dp", "chan")
f32, bf16 = jnp.float32, jnp.bfloat16
SMEM = pl.BlockSpec(memory_space=pltpu.SMEM)
VMEM = pl.BlockSpec(memory_space=pltpu.VMEM)
NN = (((1,), (0,)), ((), ()))
NT = (((1,), (1,)), ((), ()))


def gray(number):
    return number ^ (number >> 1)


def pair_bits(bits):
    stages = []
    for start in range(0, len(bits), 2):
        pair = bits[start : start + 2]
        stages.append([pair[0]] if len(pair) == 1 else [pair[0], pair[1], pair[0] ^ pair[1]])
    return stages


class Plan:
    def __init__(self, mesh, crop_shape, out_shape):
        self.n_dp, self.n_chan = mesh.shape["dp"], mesh.shape["chan"]
        self.n_all = self.n_dp * self.n_chan
        self.held, self.in_own = crop_shape[0], crop_shape[1]
        self.out_own = out_shape[1]
        self.n_in, self.n_out = self.in_own * self.n_chan, self.out_own * self.n_chan
        self.n_crops = self.held * self.n_dp
        self.strips = self.n_chan // self.held
        self.rows = -(-SIDE // self.strips)
        self.cells, self.cells_halo = self.rows * SIDE, (self.rows + 2) * SIDE
        self.strip_of = [0] * self.strips
        for strip in range(self.strips):
            self.strip_of[gray(strip)] = strip
        self.parts = 2 if (self.out_own // 2) % 8 == 0 else 1
        self.part = self.out_own // self.parts
        self.core_mask = self.n_chan
        self.strip_bits = [1 << k for k in range(self.strips.bit_length() - 1)]
        self.crop_bits = [1 << k for k in range(self.n_chan.bit_length() - 1) if (1 << k) >= self.strips]
        self.chan_bits = self.strip_bits + self.crop_bits
        self.far_bits = [self.n_chan << k for k in range(1, self.n_dp.bit_length() - 1)]
        self.dp_bits = [1 << k for k in range(self.n_dp.bit_length() - 1)]
        self.quick = self.strips == 4


def swap(block, mask, plan):
    return lax.ppermute(block, BOTH, [(i, i ^ mask) for i in range(plan.n_all)])


def split(values):
    top = values.astype(bf16)
    return top, (values - top.astype(f32)).astype(bf16)


def dot3(left, right, dims):
    (left_top, left_low), (right_top, right_low) = left, right
    dot = functools.partial(lax.dot_general, dimension_numbers=dims, preferred_element_type=f32)
    return dot(left_top, right_top) + dot(left_low, right_top) + dot(left_top, right_low)


def device_at():
    return lax.axis_index("dp"), lax.axis_index("chan")


def crop_strip(plan, dp_at, chan_at):
    low = chan_at & (plan.strips - 1)
    strip = low
    for k in range(1, plan.strips.bit_length() - 1):
        strip = strip ^ (low >> k)
    return dp_at * plan.held + chan_at // plan.strips, strip


def side_of(class_ref, crop):
    return jnp.where(class_ref[crop] == 0, SIDE, H_SMALL)


def group_cells(plan, group_ref, class_ref, crop):
    total = jnp.int32(0)
    for other in range(plan.n_crops):
        side = side_of(class_ref, other)
        total = total + jnp.where(group_ref[other] == group_ref[crop], side * side, 0)
    return total.astype(f32)


def inside_mask(plan, class_ref, crop, strip, columns, halo):
    side = side_of(class_ref, crop)
    col = lax.broadcasted_iota(jnp.int32, (SIDE, columns), 0)
    in_cols = jnp.where(col < side, 1.0, 0.0).astype(f32)
    rows = range(-1, plan.rows + 1) if halo else range(plan.rows)
    pieces = []
    for row in rows:
        at = strip * plan.rows + row
        pieces.append(in_cols * jnp.where((at >= 0) & (at < side), 1.0, 0.0).astype(f32))
    return jnp.concatenate(pieces, axis=0)


def shifted_columns(values):
    length = values.shape[0]
    col = lax.broadcasted_iota(jnp.int32, values.shape, 0) % SIDE
    left = jnp.where(col == 0, 0.0, jnp.roll(values, 1, 0))
    right = jnp.where(col == SIDE - 1, 0.0, jnp.roll(values, -1, 0))
    return left, values, right


def fill_taps(plan, values, even, odd):
    for b, moved in enumerate(shifted_columns(values)):
        top, low = split(moved)
        even[0, b], even[1, b] = top, low
        top, low = split(moved[SIDE : SIDE + plan.cells])
        odd[0, b], odd[1, b] = top, low


def read_tap(plan, even, odd, a, b):
    if a == 1:
        return odd[0, b], odd[1, b]
    start = 2 * SIDE if a == 2 else 0
    return even[0, b, start : start + plan.cells], even[1, b, start : start + plan.cells]


def tap_scratch(plan, columns):
    return [
        pltpu.VMEM((2, 3, plan.cells_halo, columns), bf16),
        pltpu.VMEM((2, 3, plan.cells, columns), bf16),
    ]


def fill_weight(plan, masks, refs, weight):
    dp_at, chan_at = device_at()
    for q, ref in enumerate(refs):
        part_at = ((dp_at & 1) ^ q) * plan.part if plan.parts > 1 else 0
        for j, mask in enumerate(masks):
            first = pl.multiple_of((chan_at ^ mask) * plan.out_own + part_at, 8)
            for t in range(TAPS):
                weight[t, pl.ds(first, plan.part), :] = ref[j, t * plan.part : (t + 1) * plan.part, :]


def fill_flat(plan, masks, refs, start, flat):
    dp_at, chan_at = device_at()
    for q, ref in enumerate(refs):
        part_at = ((dp_at & 1) ^ q) * plan.part if plan.parts > 1 else 0
        for j, mask in enumerate(masks):
            first = pl.multiple_of((chan_at ^ mask) * plan.out_own + part_at, 8)
            flat[pl.ds(first, plan.part), :] = ref[j, start : start + plan.part, :]


def conv_forward(plan, even, odd, weight):
    total = None
    for a in range(3):
        for b in range(3):
            term = dot3(read_tap(plan, even, odd, a, b), split(weight[3 * a + b]), NT)
            total = term if total is None else total + term
    return total


def conv_backward(plan, even, odd, weight):
    total = None
    for a in range(3):
        for b in range(3):
            term = dot3(read_tap(plan, even, odd, 2 - a, 2 - b), split(weight[3 * a + b]), NN)
            total = term if total is None else total + term
    return total


def row_sum(values):
    return jnp.sum(values, axis=0, keepdims=True)


def tile(rows, columns):
    blank = jnp.zeros((8 - len(rows), columns), f32)
    return jnp.concatenate(list(rows) + [blank], axis=0)


def local_stats(plan, class_ref, crop, strip, values, inside):
    side = side_of(class_ref, crop)
    cells = (jnp.clip(side - strip * plan.rows, 0, plan.rows) * side).astype(f32)
    mean = row_sum(values * inside) / jnp.maximum(cells, 1.0)
    centered = (values - mean) * inside
    return tile([mean, row_sum(centered * centered)], values.shape[1])


def write_messages(strip, stats, values, messages):
    alone, with_a, with_b = messages
    alone[...] = stats
    first, last = values[:SIDE], values[-SIDE:]
    with_a[:8] = stats
    with_b[:8] = stats
    with_a[8:] = jnp.where((strip & 1) == 0, last, first)
    with_b[8:] = jnp.where(strip == 1, last, first)


def with_edges(plan, strip, values, edge_a, edge_b):
    a, b = edge_a[8:], edge_b[8:]
    if plan.quick:
        a_above = (strip & 1) == 1
        above, below = jnp.where(a_above, a, b), jnp.where(a_above, b, a)
    else:
        above, below = a, b
    return jnp.concatenate([above, values, below], axis=0)


def crop_entries(plan, refs, masks):
    dp_at, chan_at = device_at()
    me = dp_at * plan.n_chan + chan_at
    entries, k = [], 0
    for ref in refs:
        for at in range(ref.shape[0] // 8):
            other = me ^ masks[k]
            crop, _ = crop_strip(plan, other // plan.n_chan, other % plan.n_chan)
            entries.append((crop, ref[8 * at : 8 * at + 8]))
            k += 1
    return entries


def group_stats(plan, group_ref, class_ref, crop, entries):
    count = group_cells(plan, group_ref, class_ref, crop)
    weights, mean = [], 0.0
    for other, block in entries:
        side = side_of(class_ref, other)
        same = jnp.where(group_ref[other] == group_ref[crop], 1.0, 0.0).astype(f32)
        cells = (side * side).astype(f32)
        weights.append((same, same * cells))
        mean = mean + (same * cells) * block[0:1]
    mean = mean / count
    total = 0.0
    for (same, cells), (other, block) in zip(weights, entries):
        spread = block[0:1] - mean
        total = total + same * block[1:2] + cells * (spread * spread)
    return mean, lax.rsqrt(total / count + norm_eps)


def group_sums(plan, group_ref, crop, entries, n_rows):
    total = 0.0
    for other, block in entries:
        total = total + jnp.where(group_ref[other] == group_ref[crop], 1.0, 0.0).astype(f32) * block[0:n_rows]
    return total


def sigmoid(values):
    return 1.0 / (1.0 + jnp.exp(-values))


def silu(values):
    return values * sigmoid(values)


def silu_slope(values):
    sig = sigmoid(values)
    return sig * (1.0 + values * (1.0 - sig))


def crop_inside(plan, class_ref, dp_at, which, shape):
    side = side_of(class_ref, dp_at * plan.held + which)
    at = lax.broadcasted_iota(jnp.int32, shape, 1)
    row = at // SIDE
    return jnp.where((row < side) & (at - row * SIDE < side), 1.0, 0.0).astype(f32)


def stats_kernel(plan, class_ref, maps, out):
    dp_at, _ = device_at()
    for which in range(plan.held):
        inside = crop_inside(plan, class_ref, dp_at, which, maps.shape[1:])
        side = side_of(class_ref, dp_at * plan.held + which)
        cells = (side * side).astype(f32)
        values = maps[which] * inside
        mean = jnp.sum(values, axis=1, keepdims=True) / cells
        centered = (values - mean) * inside
        squares = jnp.sum(centered * centered, axis=1, keepdims=True)
        out[0, which] = jnp.broadcast_to(mean, (plan.in_own, 128))
        out[1, which] = jnp.broadcast_to(squares, (plan.in_own, 128))


def pack_strips(plan, values, which, send):
    blank = jnp.zeros((values.shape[0], SIDE), f32)
    tail = plan.strips * plan.rows - SIDE + 1
    padded = jnp.concatenate([blank, values] + [blank] * tail, axis=1)
    for strip in range(plan.strips):
        first = strip * plan.cells
        send[which * plan.strips + gray(strip)] = padded[:, first : first + plan.cells_halo]


def norm_kernel(plan, masks, group_ref, class_ref, maps, *refs):
    parts, (norm, scales, send) = refs[:-3], refs[-3:]
    dp_at, _ = device_at()
    entries, k = [], 0
    for ref in parts:
        for block in range(ref.shape[0] // 2):
            for which in range(plan.held):
                entries.append(((dp_at ^ masks[k]) * plan.held + which, ref, block, which))
            k += 1
    for which in range(plan.held):
        crop = dp_at * plan.held + which
        count = group_cells(plan, group_ref, class_ref, crop)
        mean, total = 0.0, 0.0
        for other, ref, block, held in entries:
            side = side_of(class_ref, other)
            weight = jnp.where(group_ref[other] == group_ref[crop], side * side, 0).astype(f32)
            mean = mean + weight * ref[2 * block, held]
        mean = mean / count
        for other, ref, block, held in entries:
            side = side_of(class_ref, other)
            same = group_ref[other] == group_ref[crop]
            spread = ref[2 * block, held] - mean
            total = total + jnp.where(same, 1.0, 0.0).astype(f32) * ref[2 * block + 1, held]
            total = total + jnp.where(same, side * side, 0).astype(f32) * (spread * spread)
        scale = lax.rsqrt(total / count + norm_eps)
        scales[which] = scale
        inside = crop_inside(plan, class_ref, dp_at, which, maps.shape[1:])
        values = (maps[which] * inside - mean[:, :1]) * inside * scale[:, :1]
        norm[which] = values
        pack_strips(plan, values, which, send)


def top_kernel(plan, class_ref, top, send):
    dp_at, _ = device_at()
    for which in range(plan.held):
        inside = crop_inside(plan, class_ref, dp_at, which, top.shape[1:])
        pack_strips(plan, top[which] * inside, which, send)


def first_kernel(plan, masks, class_ref, recv, *refs):
    n = plan.parts
    packets, refs = refs[:n], refs[n:]
    entry_norm, gains, first_out, alone, with_a, with_b, weight, even, odd = refs
    dp_at, chan_at = device_at()
    crop, strip = crop_strip(plan, dp_at, chan_at)
    rows = TAPS * plan.part + plan.part
    table = packets[0][0, rows : rows + 16]
    for j in range(1, plan.n_chan):
        table = table + packets[0][j, rows : rows + 16]
    gains[...] = table
    fill_weight(plan, masks, packets, weight)
    norm = recv[...].T
    entry_norm[...] = norm
    inside = inside_mask(plan, class_ref, crop, strip, plan.n_in, True)
    pre = norm * table[0:1] + table[1:2]
    fill_taps(plan, silu(pre) * inside, even, odd)
    out = conv_forward(plan, even, odd, weight)
    first_out[...] = out
    inside = inside_mask(plan, class_ref, crop, strip, plan.n_out, False)
    write_messages(strip, local_stats(plan, class_ref, crop, strip, out, inside), out, (alone, with_a, with_b))


def wide_rows(gains):
    return [jnp.concatenate([gains[4 + 2 * k : 5 + 2 * k], gains[5 + 2 * k : 6 + 2 * k]], axis=1) for k in range(5)]


def hidden_kernel(plan, masks, crop_masks, group_ref, class_ref, gains, first_out, edge_a, edge_b, entry_norm, *refs):
    n, m = plan.parts, plan.parts * 2
    narrow_packets, packets = refs[:n], refs[n:m]
    refs = refs[m:]
    tiles, refs = refs[:-10], refs[-10:]
    middle_norm, norm_rows, hidden, alone, with_a, with_b, weight, flat, even, odd = refs
    dp_at, chan_at = device_at()
    crop, strip = crop_strip(plan, dp_at, chan_at)
    wide = wide_rows(gains)
    mean, scale = group_stats(plan, group_ref, class_ref, crop, crop_entries(plan, tiles, crop_masks))
    norm_rows[...] = tile([mean, scale], plan.n_out)
    inside = inside_mask(plan, class_ref, crop, strip, plan.n_out, True)
    norm = (with_edges(plan, strip, first_out[...], edge_a, edge_b) - mean) * inside * scale
    middle_norm[...] = norm
    fill_taps(plan, silu(norm * wide[0] + wide[1]) * inside, even, odd)
    fill_weight(plan, masks, packets, weight)
    fill_flat(plan, masks, narrow_packets, TAPS * plan.part, flat)
    inside = inside[SIDE : SIDE + plan.cells]
    shortcut_in = (entry_norm[SIDE : SIDE + plan.cells] * gains[2:3] + gains[3:4]) * inside[:, : plan.n_in]
    out = conv_forward(plan, even, odd, weight) + dot3(split(shortcut_in), split(flat[...]), NT)
    out = out * inside
    hidden[...] = out
    write_messages(strip, local_stats(plan, class_ref, crop, strip, out, inside), out, (alone, with_a, with_b))


def top_back_kernel(plan, masks, recv, *refs):
    packets, (top_halo, out, weight, even, odd) = refs[: plan.parts], refs[plan.parts :]
    top = recv[...].T
    top_halo[...] = top
    fill_taps(plan, top, even, odd)
    fill_weight(plan, masks, packets, weight)
    out[...] = conv_backward(plan, even, odd, weight)


def decoder_kernel(plan, masks, crop_masks, group_ref, class_ref, gains, hidden, edge_a, edge_b, top_back, *refs):
    packets, refs = refs[: plan.parts], refs[plan.parts :]
    tiles, refs = refs[:-7], refs[-7:]
    decoder_norm, norm_rows, pre_grad, alone, with_a, with_b, style = refs
    dp_at, chan_at = device_at()
    crop, strip = crop_strip(plan, dp_at, chan_at)
    wide = wide_rows(gains)
    entries = crop_entries(plan, tiles, crop_masks)
    mean, scale = group_stats(plan, group_ref, class_ref, crop, entries)
    fill_flat(plan, masks, packets, TAPS * plan.part, style)
    pooled = entries[0][1][0:1]
    style_scale = lax.rsqrt(jnp.sum(pooled * pooled, axis=1, keepdims=True) + style_eps)
    style_vec = pooled * style_scale
    eight = jnp.broadcast_to(style_vec, (8, plan.n_out))
    term = lax.dot_general(eight, style[...], NT, precision=highest, preferred_element_type=f32)[0:1]
    shift = wide[3] + (term + wide[4])
    norm_rows[...] = tile(
        [mean, scale, shift, style_vec, jnp.broadcast_to(style_scale, (1, plan.n_out))], plan.n_out
    )
    inside = inside_mask(plan, class_ref, crop, strip, plan.n_out, True)
    norm = (with_edges(plan, strip, hidden[...], edge_a, edge_b) - mean) * inside * scale
    decoder_norm[...] = norm
    own = norm[SIDE : SIDE + plan.cells]
    grad = top_back[...] * silu_slope(own * wide[2] + shift) * inside[SIDE : SIDE + plan.cells]
    pre_grad[...] = grad
    write_messages(strip, tile([row_sum(grad), row_sum(grad * own)], plan.n_out), grad, (alone, with_a, with_b))


def out_kernel(plan, masks, class_ref, gains, hidden, decoder_norm, norm_rows, *refs):
    packets, (send, weight, even, odd) = refs[: plan.parts], refs[plan.parts :]
    dp_at, chan_at = device_at()
    crop, strip = crop_strip(plan, dp_at, chan_at)
    wide = wide_rows(gains)
    inside = inside_mask(plan, class_ref, crop, strip, plan.n_out, True)
    fill_taps(plan, silu(decoder_norm[...] * wide[2] + norm_rows[2:3]) * inside, even, odd)
    fill_weight(plan, masks, packets, weight)
    out = hidden[...] + conv_forward(plan, even, odd, weight) * inside[SIDE : SIDE + plan.cells]
    out = out.T
    for chan in range(plan.n_chan):
        send[chan] = out[chan * plan.out_own : (chan + 1) * plan.out_own]


def hidden_back_kernel(
    plan, masks, crop_masks, group_ref, class_ref, gains, pre_grad, edge_a, edge_b,
    decoder_norm, norm_rows, top_halo, middle_norm, *refs
):
    n, m = plan.parts, plan.parts * 2
    packets, style_packets = refs[:n], refs[n:m]
    refs = refs[m:]
    tiles, refs = refs[:-9], refs[-9:]
    hidden_grad, out, alone, with_a, with_b, weight, style, even, odd = refs
    dp_at, chan_at = device_at()
    crop, strip = crop_strip(plan, dp_at, chan_at)
    wide = wide_rows(gains)
    entries = crop_entries(plan, tiles, crop_masks)
    sums = group_sums(plan, group_ref, crop, entries, 2)
    count = group_cells(plan, group_ref, class_ref, crop)
    fill_flat(plan, masks, style_packets, TAPS * plan.part, style)
    style_vec, style_scale = norm_rows[3:4], norm_rows[4:5]
    eight = jnp.broadcast_to(entries[0][1][0:1], (8, plan.n_out))
    vec_grad = lax.dot_general(eight, style[...], NN, precision=highest, preferred_element_type=f32)[0:1]
    pooled_grad = style_scale * (vec_grad - style_vec * jnp.sum(vec_grad * style_vec, axis=1, keepdims=True))
    side = side_of(class_ref, crop)
    pooled_grad = pooled_grad / (side * side).astype(f32)
    grad = with_edges(plan, strip, pre_grad[...], edge_a, edge_b)
    inside = inside_mask(plan, class_ref, crop, strip, plan.n_out, True)
    grad = norm_rows[1:2] * wide[2] * (grad - sums[0:1] / count - decoder_norm[...] * (sums[1:2] / count))
    grad = top_halo[...] + (grad + pooled_grad) * inside
    hidden_grad[...] = grad
    fill_taps(plan, grad, even, odd)
    fill_weight(plan, masks, packets, weight)
    own = middle_norm[SIDE : SIDE + plan.cells]
    result = conv_backward(plan, even, odd, weight) * silu_slope(own * wide[0] + wide[1])
    result = result * inside[SIDE : SIDE + plan.cells]
    out[...] = result
    write_messages(strip, tile([row_sum(result), row_sum(result * own)], plan.n_out), result, (alone, with_a, with_b))


def first_back_kernel(
    plan, masks, crop_masks, group_ref, class_ref, gains, pre_grad, edge_a, edge_b,
    middle_norm, norm_rows, entry_norm, shortcut_grad, *refs
):
    packets, refs = refs[: plan.parts], refs[plan.parts :]
    tiles, refs = refs[:-6], refs[-6:]
    first_grad, sums_out, send, weight, even, odd = refs
    dp_at, chan_at = device_at()
    crop, strip = crop_strip(plan, dp_at, chan_at)
    wide = wide_rows(gains)
    sums = group_sums(plan, group_ref, crop, crop_entries(plan, tiles, crop_masks), 2)
    count = group_cells(plan, group_ref, class_ref, crop)
    grad = with_edges(plan, strip, pre_grad[...], edge_a, edge_b)
    inside = inside_mask(plan, class_ref, crop, strip, plan.n_out, True)
    grad = norm_rows[1:2] * wide[0] * (grad - sums[0:1] / count - middle_norm[...] * (sums[1:2] / count)) * inside
    first_grad[...] = grad[SIDE : SIDE + plan.cells]
    fill_taps(plan, grad, even, odd)
    fill_weight(plan, masks, packets, weight)
    own = entry_norm[SIDE : SIDE + plan.cells]
    result = conv_backward(plan, even, odd, weight) * silu_slope(own * gains[0:1] + gains[1:2])
    result = result * inside[SIDE : SIDE + plan.cells, : plan.n_in]
    other = shortcut_grad[...]
    sums_out[...] = tile(
        [row_sum(result), row_sum(result * own), row_sum(other), row_sum(other * own)], plan.n_in
    )
    joined = (result * gains[0:1] + other * gains[2:3]).T
    for chan in range(plan.n_chan):
        send[chan] = joined[chan * plan.in_own : (chan + 1) * plan.in_own]


def put_weight_rows(plan, value, t, keep, away):
    dp_at, chan_at = device_at()
    core = dp_at & 1
    for j in range(plan.n_chan):
        for q, ref in enumerate((keep, away)[: plan.parts]):
            ref[j, t * plan.part : (t + 1) * plan.part, :] = value[j, q]


def weight_grad(plan, grad, even, odd, keep, away, result):
    dp_at, chan_at = device_at()
    core = dp_at & 1
    left = split(grad.T)
    for a in range(3):
        for b in range(3):
            t = 3 * a + b
            result[...] = dot3(left, read_tap(plan, even, odd, a, b), NN)
            place_rows(plan, result, lambda ref, j: ref.at[j, t * plan.part : (t + 1) * plan.part], keep, away)


def place_rows(plan, result, target, keep, away):
    dp_at, chan_at = device_at()
    core = dp_at & 1
    for j in range(plan.n_chan):
        base = (chan_at ^ j) * plan.out_own
        if plan.parts == 1:
            target(keep, j)[...] = result[pl.ds(pl.multiple_of(base, 8), plan.part)]
            continue
        target(keep, j)[...] = result[pl.ds(pl.multiple_of(base + core * plan.part, 8), plan.part)]
        target(away, j)[...] = result[pl.ds(pl.multiple_of(base + (1 - core) * plan.part, 8), plan.part)]


def decoder_weight_kernel(plan, class_ref, gains, top_halo, decoder_norm, norm_rows, *refs):
    out, (result, even, odd) = refs[: plan.parts], refs[plan.parts :]
    dp_at, chan_at = device_at()
    crop, strip = crop_strip(plan, dp_at, chan_at)
    wide = wide_rows(gains)
    inside = inside_mask(plan, class_ref, crop, strip, plan.n_out, True)
    fill_taps(plan, silu(decoder_norm[...] * wide[2] + norm_rows[2:3]) * inside, even, odd)
    weight_grad(plan, top_halo[SIDE : SIDE + plan.cells], even, odd, out[0], out[-1], result)


def middle_weight_kernel(plan, class_ref, gains, hidden_grad, middle_norm, *refs):
    out, (result, even, odd) = refs[: plan.parts], refs[plan.parts :]
    dp_at, chan_at = device_at()
    crop, strip = crop_strip(plan, dp_at, chan_at)
    wide = wide_rows(gains)
    inside = inside_mask(plan, class_ref, crop, strip, plan.n_out, True)
    fill_taps(plan, silu(middle_norm[...] * wide[0] + wide[1]) * inside, even, odd)
    weight_grad(plan, hidden_grad[SIDE : SIDE + plan.cells], even, odd, out[0], out[-1], result)


def shortcut_kernel(plan, masks, class_ref, gains, hidden_grad, entry_norm, *refs):
    packets, refs = refs[: plan.parts], refs[plan.parts :]
    pre_grad, refs = refs[0], refs[1:]
    out, (result, flat) = refs[: plan.parts], refs[plan.parts :]
    dp_at, chan_at = device_at()
    crop, strip = crop_strip(plan, dp_at, chan_at)
    inside = inside_mask(plan, class_ref, crop, strip, plan.n_in, False)
    shortcut_in = (entry_norm[SIDE : SIDE + plan.cells] * gains[2:3] + gains[3:4]) * inside
    grad = hidden_grad[SIDE : SIDE + plan.cells]
    fill_flat(plan, masks, packets, TAPS * plan.part, flat)
    pre_grad[...] = dot3(split(grad), split(flat[...]), NN) * inside
    result[...] = dot3(split(grad.T), split(shortcut_in), NN)
    place_rows(plan, result, lambda ref, j: ref.at[j], out[0], out[-1])


def entry_weight_kernel(plan, class_ref, gains, first_grad, entry_norm, *refs):
    out, (result, even, odd) = refs[: plan.parts], refs[plan.parts :]
    dp_at, chan_at = device_at()
    crop, strip = crop_strip(plan, dp_at, chan_at)
    inside = inside_mask(plan, class_ref, crop, strip, plan.n_in, True)
    fill_taps(plan, silu(entry_norm[...] * gains[0:1] + gains[1:2]) * inside, even, odd)
    weight_grad(plan, first_grad[...], even, odd, out[0], out[-1], result)


def input_grad_kernel(plan, crop_masks, group_ref, class_ref, gains, recv, norm, scales, *refs):
    tiles, out = refs[:-1], refs[-1]
    dp_at, chan_at = device_at()
    entries = crop_entries(plan, tiles, crop_masks)
    for which in range(plan.held):
        crop = dp_at * plan.held + which
        count = group_cells(plan, group_ref, class_ref, crop)
        sums = group_sums(plan, group_ref, crop, entries, 4) / count
        shift = sums[0:1] * gains[0:1] + sums[2:3] * gains[2:3]
        slope = sums[1:2] * gains[0:1] + sums[3:4] * gains[2:3]
        first = pl.ds(pl.multiple_of(chan_at * plan.in_own, plan.in_own), plan.in_own)
        turned = jnp.concatenate([shift, slope, jnp.zeros((126, plan.n_in), f32)], axis=0).T
        lanes = lax.broadcasted_iota(jnp.int32, (plan.in_own, plan.n_in), 1)
        picked = lax.broadcasted_iota(jnp.int32, (plan.in_own, plan.n_in), 0) + chan_at * plan.in_own
        pick = jnp.where(lanes == picked, 1.0, 0.0).astype(f32)
        shift = jnp.sum(pick * shift, axis=1, keepdims=True)
        slope = jnp.sum(pick * slope, axis=1, keepdims=True)
        pieces = [recv[which * plan.strips + gray(strip)] for strip in range(plan.strips)]
        joined = jnp.concatenate(pieces, axis=1)[:, : SIDE * SIDE]
        inside = crop_inside(plan, class_ref, dp_at, which, joined.shape)
        out[which] = scales[which][:, :1] * (joined - shift - norm[which] * slope) * inside


def join_kernel(plan, recv, out):
    for which in range(plan.held):
        pieces = [recv[which * plan.strips + gray(strip)] for strip in range(plan.strips)]
        out[which] = jnp.concatenate(pieces, axis=1)[:, : SIDE * SIDE]


def run(kernel, smem, arrays, out_shapes, scratch=(), flops=0):
    shapes = [jax.ShapeDtypeStruct(shape, f32) for shape in out_shapes]
    moved = 4 * sum(int(a.size) for a in arrays) + 4 * sum(int(s.size) for s in shapes)
    return pl.pallas_call(
        kernel,
        out_shape=shapes,
        in_specs=[SMEM] * len(smem) + [VMEM] * len(arrays),
        out_specs=[VMEM] * len(shapes),
        scratch_shapes=list(scratch),
        cost_estimate=pl.CostEstimate(flops=flops, bytes_accessed=moved, transcendentals=0),
        compiler_params=pltpu.CompilerParams(vmem_limit_bytes=48 * 2**20),
    )(*smem, *arrays)


def adamw(weight, gradient, moment, square, rate, decay):
    first_new = beta_one * moment + (1.0 - beta_one) * gradient
    second_new = beta_two * square + (1.0 - beta_two) * gradient * gradient
    corrected_first = first_new / (1.0 - beta_one**STEP)
    corrected_second = second_new / (1.0 - beta_two**STEP)
    updated = weight - rate * (
        corrected_first / (jnp.sqrt(corrected_second) + adam_eps) + decay * weight
    )
    return (updated, first_new, second_new)


def make_body(mesh):
    def body(
        crop_maps, out_cotangent, norm_group, scale_class,
        entry_conv, middle_conv, shortcut_map, decoder_conv, style_map, narrow_gain_table, wide_gain_table,
        entry_moment, middle_moment, shortcut_moment, decoder_moment, style_moment, narrow_moment, wide_moment,
        entry_square, middle_square, shortcut_square, decoder_square, style_square, narrow_square, wide_square,
    ):
        plan = Plan(mesh, crop_maps.shape, out_cotangent.shape)
        n_in, n_out, n_chan = plan.n_in, plan.n_out, plan.n_chan
        cells, cells_halo, part = plan.cells, plan.cells_halo, plan.part
        dp_at, chan_at = lax.axis_index("dp"), lax.axis_index("chan")
        core = dp_at & 1
        ids = (norm_group, scale_class)

        def own_part(weight):
            if plan.parts == 1:
                return weight
            return lax.dynamic_slice_in_dim(weight, core * part, part, 0)

        def tap_rows(weight):
            return jnp.transpose(own_part(weight), (1, 0, 2)).reshape(TAPS * part, weight.shape[2])

        chan_stages = pair_bits(plan.chan_bits[::-1])

        def gather_packet(packet):
            gathered, masks = packet[None], [0]
            for stage in chan_stages:
                arrived = [swap(gathered, mask, plan) for mask in stage]
                gathered = jnp.concatenate([gathered] + arrived, axis=0)
                masks = masks + [held ^ mask for mask in stage for held in masks]
            if plan.parts == 1:
                return [gathered], masks
            return [gathered, swap(gathered, plan.core_mask, plan)], masks

        narrow_tile = lax.dynamic_update_slice(
            jnp.zeros((4, n_in), f32), narrow_gain_table, (jnp.int32(0), chan_at * plan.in_own)
        )
        wide_tile = lax.dynamic_update_slice(
            jnp.zeros((5, n_out), f32), wide_gain_table, (jnp.int32(0), chan_at * plan.out_own)
        )
        gain_rows = jnp.concatenate(
            [narrow_tile, wide_tile.reshape(10, n_in), jnp.zeros((2, n_in), f32)], axis=0
        )
        packet_a, masks = gather_packet(
            jnp.concatenate([tap_rows(entry_conv), own_part(shortcut_map), gain_rows], axis=0)
        )
        packet_b, _ = gather_packet(tap_rows(middle_conv))
        packet_c, _ = gather_packet(jnp.concatenate([tap_rows(decoder_conv), own_part(style_map)], axis=0))

        def dp_swap(block, mask):
            return lax.ppermute(block, "dp", [(i, i ^ mask) for i in range(plan.n_dp)])

        def gather_strips(messages, values):
            alone, with_a, with_b = messages
            if plan.quick:
                a, b = swap(with_a, plan.strip_bits[0], plan), swap(with_b, plan.strip_bits[1], plan)
                far = swap(alone, plan.strip_bits[0] ^ plan.strip_bits[1], plan)
                return [alone, a[:8], b[:8], far], [0, 1, 2, 3], a, b
            tiles, strip_masks = [alone], [0]
            for bit in plan.strip_bits:
                stacked = jnp.concatenate(tiles, axis=0)
                stacked = swap(stacked, bit, plan)
                tiles = tiles + [stacked[8 * k : 8 * k + 8] for k in range(len(tiles))]
                strip_masks = strip_masks + [mask ^ bit for mask in strip_masks]
            up, down = [], []
            for device in range(plan.n_all):
                low = (device % n_chan) % plan.strips
                strip, base = plan.strip_of[low], device - low
                if strip + 1 < plan.strips:
                    down.append((device, base + gray(strip + 1)))
                if strip > 0:
                    up.append((device, base + gray(strip - 1)))
            blank = jnp.zeros((8, values.shape[1]), f32)
            above = lax.ppermute(values[-SIDE:], BOTH, down)
            below = lax.ppermute(values[:SIDE], BOTH, up)
            return tiles, strip_masks, jnp.concatenate([blank, above]), jnp.concatenate([blank, below])

        def gather_crops(block):
            gathered, crop_masks = [block], [0]
            stages = [[plan.core_mask]] + pair_bits(plan.crop_bits + plan.far_bits)
            for stage in stages:
                joined = gathered[0] if len(gathered) == 1 else jnp.concatenate(gathered, axis=0)
                gathered = [joined] + [swap(joined, mask, plan) for mask in stage]
                crop_masks = crop_masks + [held ^ mask for mask in stage for held in crop_masks]
            return gathered, crop_masks

        own_crop = dp_at * plan.held + chan_at // plan.strips
        own_side = jnp.where(scale_class[own_crop] == 0, SIDE, H_SMALL)

        def strip_cells(mask):
            strip = jnp.array(plan.strip_of, jnp.int32)[(chan_at ^ mask) % plan.strips]
            return (jnp.clip(own_side - strip * plan.rows, 0, plan.rows) * own_side).astype(f32)

        def merge_stats(tiles, strip_masks):
            counts = [strip_cells(mask) for mask in strip_masks]
            mean = sum(n * t[0:1] for n, t in zip(counts, tiles)) / (own_side * own_side).astype(f32)
            squares = sum(t[1:2] + n * (t[0:1] - mean) * (t[0:1] - mean) for n, t in zip(counts, tiles))
            return jnp.concatenate([mean, squares, jnp.zeros((6, mean.shape[1]), f32)], axis=0)

        def merge_sums(tiles):
            return sum(tiles)

        message_shapes = [(8, n_out), (8 + SIDE, n_out), (8 + SIDE, n_out)]
        wide_weight, wide_taps = pltpu.VMEM((TAPS, n_out, n_out), f32), tap_scratch(plan, n_out)
        narrow_weight, narrow_taps = pltpu.VMEM((TAPS, n_out, n_in), f32), tap_scratch(plan, n_in)
        flat_narrow = pltpu.VMEM((n_out, n_in), f32)
        flat_wide = pltpu.VMEM((n_out, n_out), f32)
        wide_flops = 2 * 3 * TAPS * cells * n_out * n_out
        narrow_flops = 2 * 3 * TAPS * cells * n_out * n_in

        maps_shape = crop_maps.shape
        stats = run(
            functools.partial(stats_kernel, plan), (scale_class,), (crop_maps,),
            [(2, plan.held, plan.in_own, 128)],
        )[0]
        dp_tiles, dp_masks = [stats], [0]
        for stage in pair_bits(plan.dp_bits):
            joined = dp_tiles[0] if len(dp_tiles) == 1 else jnp.concatenate(dp_tiles, axis=0)
            dp_tiles = [joined] + [dp_swap(joined, mask) for mask in stage]
            dp_masks = dp_masks + [held ^ mask for mask in stage for held in dp_masks]
        norm_held, scales, send = run(
            functools.partial(norm_kernel, plan, dp_masks), ids, (crop_maps, *dp_tiles),
            [maps_shape, (plan.held, plan.in_own, 128), (n_chan, plan.in_own, cells_halo)],
        )
        recv = lax.all_to_all(send, "chan", 0, 0).reshape(n_in, cells_halo)

        entry_norm, gains, first_out, *messages = run(
            functools.partial(first_kernel, plan, masks), (scale_class,), (recv, *packet_a),
            [(cells_halo, n_in), (16, n_in), (cells, n_out)] + message_shapes,
            [narrow_weight] + narrow_taps, narrow_flops,
        )
        tiles, strip_masks, edge_a, edge_b = gather_strips(messages, first_out)
        crop_tiles, crop_masks = gather_crops(merge_stats(tiles, strip_masks))

        middle_norm, middle_rows, hidden, *messages = run(
            functools.partial(hidden_kernel, plan, masks, crop_masks), ids,
            (gains, first_out, edge_a, edge_b, entry_norm, *packet_a, *packet_b, *crop_tiles),
            [(cells_halo, n_out), (8, n_out), (cells, n_out)] + message_shapes,
            [wide_weight, flat_narrow] + wide_taps, wide_flops,
        )
        tiles, strip_masks, edge_a, edge_b = gather_strips(messages, hidden)
        pooled_tiles, _ = gather_crops(merge_stats(tiles, strip_masks))

        top_send = run(
            functools.partial(top_kernel, plan), (scale_class,), (out_cotangent,),
            [(n_chan, plan.out_own, cells_halo)],
        )[0]
        top_recv = lax.all_to_all(top_send, "chan", 0, 0).reshape(n_out, cells_halo)
        top_halo, top_back = run(
            functools.partial(top_back_kernel, plan, masks), (), (top_recv, *packet_c),
            [(cells_halo, n_out), (cells, n_out)], [wide_weight] + wide_taps, wide_flops,
        )

        decoder_norm, decoder_rows, decoder_pre_grad, *messages = run(
            functools.partial(decoder_kernel, plan, masks, crop_masks), ids,
            (gains, hidden, edge_a, edge_b, top_back, *packet_c, *pooled_tiles),
            [(cells_halo, n_out), (8, n_out), (cells, n_out)] + message_shapes,
            [flat_wide],
        )
        tiles, strip_masks, edge_a, edge_b = gather_strips(messages, decoder_pre_grad)
        decoder_tiles, _ = gather_crops(merge_sums(tiles))

        out_send = run(
            functools.partial(out_kernel, plan, masks), (scale_class,),
            (gains, hidden, decoder_norm, decoder_rows, *packet_c),
            [(n_chan, plan.out_own, cells)], [wide_weight] + wide_taps, wide_flops,
        )[0]
        out_recv = lax.all_to_all(out_send, "chan", 0, 0)
        block_out = run(functools.partial(join_kernel, plan), (), (out_recv,), [out_cotangent.shape])[0]
        wide_packet, narrow_packet = (n_chan, TAPS * part, n_out), (n_chan, TAPS * part, n_in)
        decoder_wgrad = run(
            functools.partial(decoder_weight_kernel, plan), (scale_class,),
            (gains, top_halo, decoder_norm, decoder_rows), [wide_packet] * plan.parts, [flat_wide] + wide_taps, wide_flops,
        )

        hidden_grad, middle_pre_grad, *messages = run(
            functools.partial(hidden_back_kernel, plan, masks, crop_masks), ids,
            (gains, decoder_pre_grad, edge_a, edge_b, decoder_norm, decoder_rows, top_halo, middle_norm,
             *packet_b, *packet_c, *decoder_tiles),
            [(cells_halo, n_out), (cells, n_out)] + message_shapes,
            [wide_weight, flat_wide] + wide_taps, wide_flops,
        )
        tiles, strip_masks, edge_a, edge_b = gather_strips(messages, middle_pre_grad)
        middle_tiles, _ = gather_crops(merge_sums(tiles))
        shortcut_grad, *shortcut_wgrad = run(
            functools.partial(shortcut_kernel, plan, masks), (scale_class,), (gains, hidden_grad, entry_norm, *packet_a),
            [(cells, n_in)] + [(n_chan, part, n_in)] * plan.parts, [flat_narrow, flat_narrow],
            2 * wide_flops // (TAPS * 2),
        )
        middle_wgrad = run(
            functools.partial(middle_weight_kernel, plan), (scale_class,), (gains, hidden_grad, middle_norm),
            [wide_packet] * plan.parts, [flat_wide] + wide_taps, wide_flops,
        )

        first_grad, entry_sums, send = run(
            functools.partial(first_back_kernel, plan, masks, crop_masks), ids,
            (gains, middle_pre_grad, edge_a, edge_b, middle_norm, middle_rows, entry_norm, shortcut_grad,
             *packet_a, *middle_tiles),
            [(cells, n_out), (8, n_in), (n_chan, plan.in_own, cells)],
            [narrow_weight] + wide_taps, narrow_flops,
        )
        entry_wgrad = run(
            functools.partial(entry_weight_kernel, plan), (scale_class,), (gains, first_grad, entry_norm),
            [narrow_packet] * plan.parts, [flat_narrow] + narrow_taps, narrow_flops,
        )
        recv = lax.all_to_all(send, "chan", 0, 0)
        entry_block, entry_masks = [entry_sums], [0]
        strip_total = entry_sums
        for stage in pair_bits(plan.strip_bits):
            strip_total = strip_total + sum(swap(strip_total, mask, plan) for mask in stage)
        entry_tiles, _ = gather_crops(strip_total)
        input_grad = run(
            functools.partial(input_grad_kernel, plan, crop_masks), ids,
            (gains, recv, norm_held, scales, *entry_tiles), [maps_shape],
        )[0]

        def reduce_packet(grads):
            total = grads[0]
            if plan.parts == 2:
                total = total + swap(grads[1], plan.core_mask, plan)
            blocks = [total[j] for j in range(n_chan)]
            for bit in plan.chan_bits[:1]:
                sent = jnp.stack([blocks[j] for j in range(n_chan) if j & bit])
                arrived = swap(sent, bit, plan)
                blocks = [blocks[2 * k] + arrived[k] for k in range(n_chan // 2)]
            total = blocks[0]
            for k in range(1, len(blocks)):
                total = total + swap(blocks[k], 2 * k, plan)
            for bit in plan.far_bits + ([plan.core_mask] if plan.parts == 1 else []):
                total = total + swap(total, bit, plan)
            if plan.parts == 1:
                return [total]
            other = swap(total, plan.core_mask, plan)
            return [jnp.where(core == 0, total, other), jnp.where(core == 0, other, total)]

        def from_taps(pieces):
            width = pieces[0].shape[-1]
            return jnp.concatenate(
                [jnp.transpose(p.reshape(TAPS, part, width), (1, 0, 2)) for p in pieces], axis=0
            )

        decoder_sum = from_taps(reduce_packet(decoder_wgrad))
        middle_sum = from_taps(reduce_packet(middle_wgrad))
        shortcut_sum = jnp.concatenate(reduce_packet(shortcut_wgrad), axis=0)
        entry_sum = from_taps(reduce_packet(entry_wgrad))

        def stack_crops(tiles):
            return jnp.concatenate(tiles, axis=0).reshape(plan.n_crops, 8, -1)

        def own_columns(rows, size):
            return lax.dynamic_slice_in_dim(rows, chan_at * size, size, 1)

        pooled_all, decoder_all = stack_crops(pooled_tiles)[:, 0], stack_crops(decoder_tiles)
        style_vecs = pooled_all * lax.rsqrt(jnp.sum(pooled_all * pooled_all, axis=1, keepdims=True) + style_eps)
        style_sum = jnp.einsum(
            "no,nc->oc", own_columns(decoder_all[:, 0], plan.out_own), style_vecs, precision=highest
        )
        decoder_total = jnp.sum(decoder_all, axis=0)
        middle_total = jnp.sum(stack_crops(middle_tiles), axis=0)
        entry_total = jnp.sum(stack_crops(entry_tiles), axis=0)
        narrow_sum = own_columns(
            jnp.stack([entry_total[1], entry_total[0], entry_total[3], entry_total[2]]), plan.in_own
        )
        wide_sum = own_columns(
            jnp.stack([middle_total[1], middle_total[0], decoder_total[1], decoder_total[0], decoder_total[0]]),
            plan.out_own,
        )

        gradients = (entry_sum, middle_sum, shortcut_sum, decoder_sum, style_sum, narrow_sum, wide_sum)
        local_squares = jnp.zeros((), f32)
        for gradient in gradients:
            local_squares = local_squares + jnp.sum(gradient * gradient)
        total_squares = jnp.broadcast_to(local_squares, (8, 128))
        for stage in pair_bits(plan.chan_bits):
            total_squares = total_squares + sum(swap(total_squares, mask, plan) for mask in stage)
        grad_norm = jnp.sqrt(total_squares[0, 0])
        clip_factor = jnp.minimum(1.0, clip_bound / grad_norm)
        params = (entry_conv, middle_conv, shortcut_map, decoder_conv, style_map, narrow_gain_table, wide_gain_table)
        moments = (
            entry_moment, middle_moment, shortcut_moment, decoder_moment, style_moment, narrow_moment, wide_moment,
        )
        squares = (
            entry_square, middle_square, shortcut_square, decoder_square, style_square, narrow_square, wide_square,
        )
        rates = (0.06, 0.04, 0.16, 0.04, 1.0, 0.4, 0.4)
        decays = (decay_rate, decay_rate, decay_rate, decay_rate, decay_rate, 0.0, 0.0)
        results = [block_out, input_grad]
        for which in range(7):
            results.extend(
                adamw(
                    params[which], gradients[which] * clip_factor, moments[which], squares[which],
                    rates[which], decays[which],
                )
            )
        return tuple(results) + (grad_norm,)

    return body


def solution(mesh):
    maps, whole = P("dp", "chan", None), P()
    conv_spec, flat_spec, table_spec = P("chan", None, None), P("chan", None), P(None, "chan")
    params = (conv_spec, conv_spec, flat_spec, conv_spec, flat_spec, table_spec, table_spec)
    updated = tuple(spec for spec in params for _ in range(3))
    return jax.shard_map(
        make_body(mesh),
        mesh=mesh,
        in_specs=(maps, maps, whole, whole) + params * 3,
        out_specs=(maps, maps) + updated + (whole,),
        check_vma=False,
    )
```

```python
import functools

import jax
import jax.numpy as jnp
from jax import lax
from jax.experimental import pallas as pl
from jax.experimental.pallas import tpu as pltpu
from jax.sharding import PartitionSpec as P

SIDE = 56
H_SMALL = 40
NGRP = 4
STEP = 10
TAPS = 9
VMEM_LIMIT = 20 * 2**20
COST = 1
TAIL = 1
STORED_MAPS, STORED_WEIGHTS = 60, 22
HIDE = 1
MIDDLE = 0

beta_one = 0.9
beta_two = 0.999
adam_eps = 1e-08
decay_rate = 0.01
clip_bound = 1.0
norm_eps = 1e-05
style_eps = 1e-06
highest = lax.Precision.HIGHEST
BOTH = ("dp", "chan")
f32, bf16 = jnp.float32, jnp.bfloat16
SMEM = pl.BlockSpec(memory_space=pltpu.SMEM)
VMEM = pl.BlockSpec(memory_space=pltpu.VMEM)
NN = (((1,), (0,)), ((), ()))
NT = (((1,), (1,)), ((), ()))


def gray(number):
    return number ^ (number >> 1)


def pair_bits(bits):
    stages = []
    for start in range(0, len(bits), 2):
        pair = bits[start : start + 2]
        stages.append([pair[0]] if len(pair) == 1 else [pair[0], pair[1], pair[0] ^ pair[1]])
    return stages


class Plan:
    def __init__(self, mesh, crop_shape, out_shape):
        self.n_dp, self.n_chan = mesh.shape["dp"], mesh.shape["chan"]
        self.n_all = self.n_dp * self.n_chan
        self.held, self.in_own = crop_shape[0], crop_shape[1]
        self.out_own = out_shape[1]
        self.n_in, self.n_out = self.in_own * self.n_chan, self.out_own * self.n_chan
        self.n_crops = self.held * self.n_dp
        self.strips = self.n_chan // self.held
        self.rows = -(-SIDE // self.strips)
        self.cells, self.cells_halo = self.rows * SIDE, (self.rows + 2) * SIDE
        self.strip_of = [0] * self.strips
        for strip in range(self.strips):
            self.strip_of[gray(strip)] = strip
        self.parts = 2 if self.out_own % 16 == 0 and self.n_dp >= 2 else 1
        self.part = self.out_own // self.parts
        self.wide_parts = 4 if self.out_own % 32 == 0 and self.n_dp >= 4 else self.parts
        self.core_mask = self.n_chan
        self.strip_bits = [1 << k for k in range(self.strips.bit_length() - 1)]
        self.chan_bits = [1 << k for k in range(self.n_chan.bit_length() - 1)]
        self.crop_bits = [1 << k for k in range(self.n_chan.bit_length() - 1) if (1 << k) >= self.strips]
        self.far_bits = [self.n_chan << k for k in range(1, self.n_dp.bit_length() - 1)]
        self.dp_bits = [1 << k for k in range(self.n_dp.bit_length() - 1)]
        self.quick = self.strips == 4

    def devices_of(self, crop):
        base = crop // self.held * self.n_chan + crop % self.held * self.strips
        return [base + gray(strip) for strip in range(self.strips)]


def swap(block, mask, plan):
    return lax.ppermute(block, BOTH, [(i, i ^ mask) for i in range(plan.n_all)])


def split(values):
    top = values.astype(bf16)
    return top, (values - top.astype(f32)).astype(bf16)


def dot3(left, right, dims):
    (left_top, left_low), (right_top, right_low) = left, right
    dot = functools.partial(lax.dot_general, dimension_numbers=dims, preferred_element_type=f32)
    return dot(left_top, right_top) + dot(left_low, right_top) + dot(left_top, right_low)


def device_at():
    return lax.axis_index("dp"), lax.axis_index("chan")


def crop_strip(plan, dp_at, chan_at):
    low = chan_at & (plan.strips - 1)
    strip = low
    for k in range(1, plan.strips.bit_length() - 1):
        strip = strip ^ (low >> k)
    return dp_at * plan.held + chan_at // plan.strips, strip


def side_of(class_ref, crop):
    return jnp.where(class_ref[crop] == 0, SIDE, H_SMALL)


def group_cells(plan, group_ref, class_ref, crop):
    total = jnp.int32(0)
    for other in range(plan.n_crops):
        side = side_of(class_ref, other)
        total = total + jnp.where(group_ref[other] == group_ref[crop], side * side, 0)
    return total.astype(f32)


def inside_mask(plan, class_ref, crop, strip, columns, halo):
    side = side_of(class_ref, crop)
    col = lax.broadcasted_iota(jnp.int32, (SIDE, columns), 0)
    in_cols = jnp.where(col < side, 1.0, 0.0).astype(f32)
    rows = range(-1, plan.rows + 1) if halo else range(plan.rows)
    pieces = []
    for row in rows:
        at = strip * plan.rows + row
        pieces.append(in_cols * jnp.where((at >= 0) & (at < side), 1.0, 0.0).astype(f32))
    return jnp.concatenate(pieces, axis=0)


def shifted_columns(values):
    length = values.shape[0]
    col = lax.broadcasted_iota(jnp.int32, values.shape, 0) % SIDE
    left = jnp.where(col == 0, 0.0, jnp.roll(values, 1, 0))
    right = jnp.where(col == SIDE - 1, 0.0, jnp.roll(values, -1, 0))
    return left, values, right


def fill_taps(plan, values, even, odd):
    for b, moved in enumerate(shifted_columns(values)):
        top, low = split(moved)
        even[0, b], even[1, b] = top, low
        top, low = split(moved[SIDE : SIDE + plan.cells])
        odd[0, b], odd[1, b] = top, low


def read_tap(plan, even, odd, a, b):
    if a == 1:
        return odd[0, b], odd[1, b]
    start = 2 * SIDE if a == 2 else 0
    return even[0, b, start : start + plan.cells], even[1, b, start : start + plan.cells]


def tap_scratch(plan, columns):
    return [
        pltpu.VMEM((2, 3, plan.cells_halo, columns), bf16),
        pltpu.VMEM((2, 3, plan.cells, columns), bf16),
    ]


class Packet:
    def __init__(self, arrays, senders, parts, base=0):
        self.arrays, self.senders, self.parts, self.base = arrays, senders, parts, base

    def scratch(self, plan, taps, columns):
        n, part = sum(len(chans or [0]) for _, chans in self.senders), plan.out_own // self.parts
        return [
            pltpu.VMEM((plan.n_chan, self.parts, taps, part, columns), f32), pltpu.SemaphoreType.DMA((n,))
        ]

    def load(self, plan, refs, first, taps, weight, sems):
        dp_at, chan_at = device_at()
        copies, first = [], first + self.base
        for ref, (dp_mask, chans) in zip(refs, self.senders):
            place = (dp_at ^ dp_mask) & (self.parts - 1)
            if chans is None:
                pairs = [(ref.at[:, first : first + taps], weight.at[:, place])]
            else:
                pairs = [
                    (ref.at[j, first : first + taps], weight.at[chan_at ^ mask, place])
                    for j, mask in enumerate(chans)
                ]
            for source, target in pairs:
                copy = pltpu.make_async_copy(source, target, sems.at[len(copies)])
                copy.start()
                copies.append(copy)
        return copies


def wait_all(copies):
    for copy in copies:
        copy.wait()


def tap_weight(weight, t):
    block = weight[:, :, t]
    return block.reshape(block.shape[0] * block.shape[1] * block.shape[2], block.shape[3])


def conv_forward(plan, even, odd, weight):
    total = None
    for a in range(3):
        for b in range(3):
            term = dot3(read_tap(plan, even, odd, a, b), split(tap_weight(weight, 3 * a + b)), NT)
            total = term if total is None else total + term
    return total


def conv_backward(plan, even, odd, weight):
    total = None
    for a in range(3):
        for b in range(3):
            term = dot3(read_tap(plan, even, odd, 2 - a, 2 - b), split(tap_weight(weight, 3 * a + b)), NN)
            total = term if total is None else total + term
    return total


def row_sum(values):
    return jnp.sum(values, axis=0, keepdims=True)


def tile(rows, columns):
    blank = jnp.zeros((8 - len(rows), columns), f32)
    return jnp.concatenate(list(rows) + [blank], axis=0)


def fold(row):
    half = row.shape[1] // 2
    return jnp.concatenate([row[:, :half], row[:, half:]], axis=0)


def unfold(pair):
    return jnp.concatenate([pair[0:1], pair[1:2]], axis=1)


def strip_cells(plan, side, strip):
    return (jnp.clip(side - strip * plan.rows, 0, plan.rows) * side).astype(f32)


def local_stats(plan, class_ref, crop, strip, values, inside):
    mean = row_sum(values * inside) / jnp.maximum(strip_cells(plan, side_of(class_ref, crop), strip), 1.0)
    centered = (values - mean) * inside
    return mean, row_sum(centered * centered)


def write_messages(plan, strip, rows, values, messages):
    everyone, edge_a, edge_b = messages
    block = jnp.concatenate([fold(row) for row in rows], axis=0)
    for device in range(plan.n_all):
        everyone[device] = block
    first, last = values[:SIDE], values[-SIDE:]
    edge_a[...] = jnp.where((strip & 1) == 0, last, first) if plan.quick else last
    edge_b[...] = jnp.where(strip == 1, last, first) if plan.quick else first


def with_edges(plan, strip, values, edge_a, edge_b):
    a, b = edge_a[...], edge_b[...]
    if plan.quick:
        a_above = (strip & 1) == 1
        above, below = jnp.where(a_above, a, b), jnp.where(a_above, b, a)
    else:
        above, below = a, b
    return jnp.concatenate([above, values, below], axis=0)


def same_group(group_ref, other, crop):
    return jnp.where(group_ref[other] == group_ref[crop], 1.0, 0.0).astype(f32)


def crop_means(plan, class_ref, stats):
    means = []
    for other in range(plan.n_crops):
        side = side_of(class_ref, other)
        mean = 0.0
        for strip, device in enumerate(plan.devices_of(other)):
            mean = mean + strip_cells(plan, side, strip) * stats[device, 0:2]
        means.append(mean / (side * side).astype(f32))
    return means


def group_stats(plan, group_ref, class_ref, crop, stats):
    count = group_cells(plan, group_ref, class_ref, crop)
    weights, mean = [], 0.0
    for other in range(plan.n_crops):
        same, side = same_group(group_ref, other, crop), side_of(class_ref, other)
        for strip, device in enumerate(plan.devices_of(other)):
            weights.append((device, same, same * strip_cells(plan, side, strip)))
            mean = mean + weights[-1][2] * stats[device, 0:2]
    mean = mean / count
    total = 0.0
    for device, same, cells in weights:
        spread = stats[device, 0:2] - mean
        total = total + same * stats[device, 2:4] + cells * (spread * spread)
    return unfold(mean), unfold(lax.rsqrt(total / count + norm_eps))


def crop_sums(plan, sums, other):
    total = 0.0
    for device in plan.devices_of(other):
        total = total + sums[device]
    return total


def group_sums(plan, group_ref, crop, sums):
    total = 0.0
    for other in range(plan.n_crops):
        total = total + same_group(group_ref, other, crop) * crop_sums(plan, sums, other)
    return unfold(total[0:2]), unfold(total[2:4])


def own_crop(plan, crop, pairs):
    total = 0.0
    for other, pair in enumerate(pairs):
        total = total + jnp.where(crop == other, pair, 0.0)
    return unfold(total)


def sigmoid(values):
    return 1.0 / (1.0 + jnp.exp(-values))


def silu(values):
    return values * sigmoid(values)


def silu_slope(values):
    sig = sigmoid(values)
    return sig * (1.0 + values * (1.0 - sig))


def crop_inside(plan, class_ref, dp_at, which, shape):
    side = side_of(class_ref, dp_at * plan.held + which)
    at = lax.broadcasted_iota(jnp.int32, shape, 1)
    row = at // SIDE
    return jnp.where((row < side) & (at - row * SIDE < side), 1.0, 0.0).astype(f32)


def stats_kernel(plan, class_ref, maps, out):
    dp_at, _ = device_at()
    for which in range(plan.held):
        inside = crop_inside(plan, class_ref, dp_at, which, maps.shape[1:])
        side = side_of(class_ref, dp_at * plan.held + which)
        cells = (side * side).astype(f32)
        values = maps[which] * inside
        mean = jnp.sum(values, axis=1, keepdims=True) / cells
        centered = (values - mean) * inside
        squares = jnp.sum(centered * centered, axis=1, keepdims=True)
        out[0, which] = jnp.broadcast_to(mean, (plan.in_own, 128))
        out[1, which] = jnp.broadcast_to(squares, (plan.in_own, 128))


def pack_strips(plan, values, which, send):
    blank = jnp.zeros((values.shape[0], SIDE), f32)
    tail = plan.strips * plan.rows - SIDE + 1
    padded = jnp.concatenate([blank, values] + [blank] * tail, axis=1)
    for strip in range(plan.strips):
        first = strip * plan.cells
        send[which * plan.strips + gray(strip)] = padded[:, first : first + plan.cells_halo]


def norm_kernel(plan, masks, group_ref, class_ref, maps, *refs):
    parts, (norm, scales, send) = refs[:-3], refs[-3:]
    dp_at, _ = device_at()
    entries, k = [], 0
    for ref in parts:
        for block in range(ref.shape[0] // 2):
            for which in range(plan.held):
                entries.append(((dp_at ^ masks[k]) * plan.held + which, ref, block, which))
            k += 1
    for which in range(plan.held):
        crop = dp_at * plan.held + which
        count = group_cells(plan, group_ref, class_ref, crop)
        mean, total = 0.0, 0.0
        for other, ref, block, held in entries:
            side = side_of(class_ref, other)
            weight = jnp.where(group_ref[other] == group_ref[crop], side * side, 0).astype(f32)
            mean = mean + weight * ref[2 * block, held]
        mean = mean / count
        for other, ref, block, held in entries:
            side = side_of(class_ref, other)
            same = group_ref[other] == group_ref[crop]
            spread = ref[2 * block, held] - mean
            total = total + jnp.where(same, 1.0, 0.0).astype(f32) * ref[2 * block + 1, held]
            total = total + jnp.where(same, side * side, 0).astype(f32) * (spread * spread)
        scale = lax.rsqrt(total / count + norm_eps)
        scales[which] = scale
        inside = crop_inside(plan, class_ref, dp_at, which, maps.shape[1:])
        values = (maps[which] * inside - mean[:, :1]) * inside * scale[:, :1]
        norm[which] = values
        pack_strips(plan, values, which, send)


def gate_kernel(*refs):
    refs[-1][...] = jnp.zeros((8, 128), f32)


def top_kernel(plan, class_ref, top, send):
    dp_at, _ = device_at()
    for which in range(plan.held):
        inside = crop_inside(plan, class_ref, dp_at, which, top.shape[1:])
        pack_strips(plan, top[which] * inside, which, send)


def first_kernel(plan, packet, class_ref, recv, *refs):
    n = len(packet.arrays)
    packets, refs = refs[:n], refs[n:]
    entry_norm, gains, first_out, shortcut, kept, everyone, edge_a, edge_b = refs[:8]
    weight, rest, sems, rest_sems, even, odd = refs[8:]
    n_tables = 16 // plan.part
    copies = packet.load(plan, packets, 0, TAPS, weight, sems)
    rest_copies = packet.load(plan, packets, TAPS, 1 + n_tables, rest, rest_sems)
    dp_at, chan_at = device_at()
    crop, strip = crop_strip(plan, dp_at, chan_at)
    norm = recv[...].T
    entry_norm[...] = norm
    inside = inside_mask(plan, class_ref, crop, strip, plan.n_in, True)
    wait_all(rest_copies)
    table = 0.0
    for j in range(plan.n_chan):
        table = table + jnp.concatenate([rest[j, 0, 1 + k] for k in range(n_tables)], axis=0)
    gains[...] = table
    shortcut[...] = tap_weight(rest, 0)
    pre = norm * table[0:1] + table[1:2]
    fill_taps(plan, silu(pre) * inside, even, odd)
    wait_all(copies)
    kept.take(weight)
    out = conv_forward(plan, even, odd, weight)
    first_out[...] = out
    inside = inside_mask(plan, class_ref, crop, strip, plan.n_out, False)
    stats = local_stats(plan, class_ref, crop, strip, out, inside)
    write_messages(plan, strip, stats, out, (everyone, edge_a, edge_b))


def wide_rows(gains):
    return [jnp.concatenate([gains[4 + 2 * k : 5 + 2 * k], gains[5 + 2 * k : 6 + 2 * k]], axis=1) for k in range(5)]


def hidden_kernel(
    plan, packet, group_ref, class_ref, gains, first_out, edge_a, edge_b, entry_norm, stats, shortcut, *refs
):
    n = len(packet.arrays)
    packets, refs = refs[:n], refs[n:]
    middle_norm, norm_rows, hidden, kept, everyone, with_a, with_b, weight, sems, even, odd = refs
    copies = packet.load(plan, packets, 0, TAPS, weight, sems)
    dp_at, chan_at = device_at()
    crop, strip = crop_strip(plan, dp_at, chan_at)
    wide = wide_rows(gains)
    mean, scale = group_stats(plan, group_ref, class_ref, crop, stats)
    norm_rows[...] = tile([mean, scale], plan.n_out)
    inside = inside_mask(plan, class_ref, crop, strip, plan.n_out, True)
    norm = (with_edges(plan, strip, first_out[...], edge_a, edge_b) - mean) * inside * scale
    middle_norm[...] = norm
    fill_taps(plan, silu(norm * wide[0] + wide[1]) * inside, even, odd)
    inside = inside[SIDE : SIDE + plan.cells]
    shortcut_in = (entry_norm[SIDE : SIDE + plan.cells] * gains[2:3] + gains[3:4]) * inside[:, : plan.n_in]
    out = dot3(split(shortcut_in), split(shortcut[...]), NT)
    wait_all(copies)
    kept.take(weight)
    out = (conv_forward(plan, even, odd, weight) + out) * inside
    hidden[...] = out
    stats = local_stats(plan, class_ref, crop, strip, out, inside)
    write_messages(plan, strip, stats, out, (everyone, with_a, with_b))


def top_back_kernel(plan, packet, recv, *refs):
    n = len(packet.arrays)
    packets, (top_halo, out, style, kept, weight, flat, sems, flat_sems, even, odd) = refs[:n], refs[n:]
    copies = packet.load(plan, packets, 0, TAPS, weight, sems)
    flat_copies = packet.load(plan, packets, TAPS, 1, flat, flat_sems)
    top = recv[...].T
    top_halo[...] = top
    fill_taps(plan, top, even, odd)
    wait_all(flat_copies)
    style[...] = tap_weight(flat, 0)
    wait_all(copies)
    kept.take(weight)
    out[...] = conv_backward(plan, even, odd, weight)


def decoder_kernel(plan, group_ref, class_ref, gains, hidden, edge_a, edge_b, top_back, stats, style, *refs):
    decoder_norm, norm_rows, pre_grad, alone, with_a, with_b = refs
    dp_at, chan_at = device_at()
    crop, strip = crop_strip(plan, dp_at, chan_at)
    wide = wide_rows(gains)
    mean, scale = group_stats(plan, group_ref, class_ref, crop, stats)
    pooled = own_crop(plan, crop, crop_means(plan, class_ref, stats))
    style_scale = lax.rsqrt(jnp.sum(pooled * pooled, axis=1, keepdims=True) + style_eps)
    style_vec = pooled * style_scale
    eight = jnp.broadcast_to(style_vec, (8, plan.n_out))
    term = lax.dot_general(eight, style[...], NT, precision=highest, preferred_element_type=f32)[0:1]
    shift = wide[3] + (term + wide[4])
    norm_rows[...] = tile(
        [mean, scale, shift, style_vec, jnp.broadcast_to(style_scale, (1, plan.n_out))], plan.n_out
    )
    inside = inside_mask(plan, class_ref, crop, strip, plan.n_out, True)
    norm = (with_edges(plan, strip, hidden[...], edge_a, edge_b) - mean) * inside * scale
    decoder_norm[...] = norm
    own = norm[SIDE : SIDE + plan.cells]
    grad = top_back[...] * silu_slope(own * wide[2] + shift) * inside[SIDE : SIDE + plan.cells]
    pre_grad[...] = grad
    write_messages(plan, strip, (row_sum(grad), row_sum(grad * own)), grad, (alone, with_a, with_b))


def out_kernel(plan, class_ref, gains, hidden, decoder_norm, norm_rows, weight, send, even, odd):
    dp_at, chan_at = device_at()
    crop, strip = crop_strip(plan, dp_at, chan_at)
    wide = wide_rows(gains)
    inside = inside_mask(plan, class_ref, crop, strip, plan.n_out, True)
    fill_taps(plan, silu(decoder_norm[...] * wide[2] + norm_rows[2:3]) * inside, even, odd)
    out = hidden[...] + conv_forward(plan, even, odd, weight) * inside[SIDE : SIDE + plan.cells]
    out = out.T
    for chan in range(plan.n_chan):
        send[chan] = out[chan * plan.out_own : (chan + 1) * plan.out_own]


def hidden_back_kernel(
    plan, group_ref, class_ref, gains, pre_grad, edge_a, edge_b,
    decoder_norm, norm_rows, top_halo, middle_norm, all_sums, style, weight, *refs
):
    hidden_grad, out, alone, with_a, with_b, even, odd = refs
    dp_at, chan_at = device_at()
    crop, strip = crop_strip(plan, dp_at, chan_at)
    wide = wide_rows(gains)
    shift, slope = group_sums(plan, group_ref, crop, all_sums)
    count = group_cells(plan, group_ref, class_ref, crop)
    style_vec, style_scale = norm_rows[3:4], norm_rows[4:5]
    own_grad = own_crop(plan, crop, [crop_sums(plan, all_sums, other)[0:2] for other in range(plan.n_crops)])
    eight = jnp.broadcast_to(own_grad, (8, plan.n_out))
    vec_grad = lax.dot_general(eight, style[...], NN, precision=highest, preferred_element_type=f32)[0:1]
    pooled_grad = style_scale * (vec_grad - style_vec * jnp.sum(vec_grad * style_vec, axis=1, keepdims=True))
    side = side_of(class_ref, crop)
    pooled_grad = pooled_grad / (side * side).astype(f32)
    grad = with_edges(plan, strip, pre_grad[...], edge_a, edge_b)
    inside = inside_mask(plan, class_ref, crop, strip, plan.n_out, True)
    grad = norm_rows[1:2] * wide[2] * (grad - shift / count - decoder_norm[...] * (slope / count))
    grad = top_halo[...] + (grad + pooled_grad) * inside
    hidden_grad[...] = grad
    fill_taps(plan, grad, even, odd)
    own = middle_norm[SIDE : SIDE + plan.cells]
    result = conv_backward(plan, even, odd, weight) * silu_slope(own * wide[0] + wide[1])
    result = result * inside[SIDE : SIDE + plan.cells]
    out[...] = result
    write_messages(plan, strip, (row_sum(result), row_sum(result * own)), result, (alone, with_a, with_b))


def first_grad_kernel(
    plan, reduction, group_ref, class_ref, gains, pre_grad, edge_a, edge_b,
    middle_norm, norm_rows, entry_norm, all_sums, *refs
):
    first_grad, keep, away, result, even, odd = refs
    dp_at, chan_at = device_at()
    crop, strip = crop_strip(plan, dp_at, chan_at)
    wide = wide_rows(gains)
    shift, slope = group_sums(plan, group_ref, crop, all_sums)
    count = group_cells(plan, group_ref, class_ref, crop)
    grad = with_edges(plan, strip, pre_grad[...], edge_a, edge_b)
    inside = inside_mask(plan, class_ref, crop, strip, plan.n_out, True)
    grad = norm_rows[1:2] * wide[0] * (grad - shift / count - middle_norm[...] * (slope / count)) * inside
    first_grad[...] = grad
    act = silu(entry_norm[...] * gains[0:1] + gains[1:2]) * inside[:, : plan.n_in]
    fill_taps(plan, act, even, odd)
    weight_grad(plan, reduction, grad[SIDE : SIDE + plan.cells], even, odd, keep, away, result)


def first_back_kernel(
    plan, class_ref, gains, first_grad, entry_norm, shortcut_grad, weight, send, even, odd
):
    dp_at, chan_at = device_at()
    crop, strip = crop_strip(plan, dp_at, chan_at)
    fill_taps(plan, first_grad[...], even, odd)
    own = entry_norm[SIDE : SIDE + plan.cells]
    result = conv_backward(plan, even, odd, weight) * silu_slope(own * gains[0:1] + gains[1:2])
    result = result * inside_mask(plan, class_ref, crop, strip, plan.n_in, False)
    other = shortcut_grad[...]
    sums = tile([row_sum(result), row_sum(result * own), row_sum(other), row_sum(other * own)], plan.n_in).T
    joined = (result * gains[0:1] + other * gains[2:3]).T
    for chan in range(plan.n_chan):
        rows = slice(chan * plan.in_own, (chan + 1) * plan.in_own)
        send[chan, :, : plan.cells] = joined[rows]
        send[chan, :, plan.cells :] = sums[rows, :4]


class Reduction:
    def __init__(self, plan, taps, parts, halving=None):
        self.taps, self.parts, self.part = taps, parts, plan.out_own // parts
        self.halving, self.masks, self.blocks = halving, None, plan.n_chan
        if halving is None:
            return
        self.last = [0]
        for bit in plan.chan_bits:
            if bit not in halving:
                self.last = self.last + [mask | bit for mask in self.last]
        self.masks = self.last
        for bit in halving[::-1]:
            self.masks = self.masks + [mask | bit for mask in self.masks]
        self.blocks = len(self.masks)

    def shape(self, columns):
        return (self.blocks, self.taps, self.part, columns)


def place_rows(plan, reduction, result, t, keep, away):
    dp_at, chan_at = device_at()
    for ref, core in ((keep, 0), (away, 1))[: plan.parts]:
        for j in range(reduction.blocks):
            if reduction.masks is None:
                owner_dp, owner = dp_at ^ core, j
            else:
                mask = reduction.masks[j]
                owner_dp, owner = dp_at ^ core ^ (mask // plan.n_chan), chan_at ^ (mask % plan.n_chan)
            first = owner * plan.out_own + (owner_dp & (reduction.parts - 1)) * reduction.part
            ref[j, t] = result[pl.ds(pl.multiple_of(first, 8), reduction.part)]


def weight_grad(plan, reduction, grad, even, odd, keep, away, result):
    left = split(grad.T)
    for a in range(3):
        for b in range(3):
            result[...] = dot3(left, read_tap(plan, even, odd, a, b), NN)
            place_rows(plan, reduction, result, 3 * a + b, keep, away)


def decoder_weight_kernel(plan, reduction, class_ref, gains, top_halo, decoder_norm, norm_rows, *refs):
    keep, away, result, even, odd = refs
    dp_at, chan_at = device_at()
    crop, strip = crop_strip(plan, dp_at, chan_at)
    wide = wide_rows(gains)
    inside = inside_mask(plan, class_ref, crop, strip, plan.n_out, True)
    fill_taps(plan, silu(decoder_norm[...] * wide[2] + norm_rows[2:3]) * inside, even, odd)
    weight_grad(plan, reduction, top_halo[SIDE : SIDE + plan.cells], even, odd, keep, away, result)


def middle_weight_kernel(
    plan, reduction, class_ref, gains, hidden_grad, middle_norm, entry_norm, shortcut, *refs
):
    shortcut_grad, keep, away, result, even, odd = refs
    dp_at, chan_at = device_at()
    crop, strip = crop_strip(plan, dp_at, chan_at)
    wide = wide_rows(gains)
    inside = inside_mask(plan, class_ref, crop, strip, plan.n_out, True)
    fill_taps(plan, silu(middle_norm[...] * wide[0] + wide[1]) * inside, even, odd)
    grad = hidden_grad[SIDE : SIDE + plan.cells]
    weight_grad(plan, reduction, grad, even, odd, keep, away, result)
    inside = inside[SIDE : SIDE + plan.cells, : plan.n_in]
    shortcut_in = (entry_norm[SIDE : SIDE + plan.cells] * gains[2:3] + gains[3:4]) * inside
    shortcut_grad[...] = dot3(split(grad), split(shortcut[...]), NN) * inside
    result[:, : plan.n_in] = dot3(split(grad.T), split(shortcut_in), NN)
    result[:, plan.n_in :] = jnp.zeros((plan.n_out, plan.n_out - plan.n_in), f32)
    place_rows(plan, reduction, result, TAPS, keep, away)


def add_kernel(count, *refs):
    left, right, outs = refs[0], refs[1], refs[2:]
    size = left.shape[0] // count
    for k, out in enumerate(outs):
        out[...] = left[k * size : (k + 1) * size] + right[k * size : (k + 1) * size]


def total_kernel(*refs):
    out = refs[-1]
    total = refs[0][...]
    for ref in refs[1:-1]:
        total = total + ref[...]
    out[...] = total


def sum_blocks_kernel(blocks, out):
    total = blocks[0]
    for k in range(1, blocks.shape[0]):
        total = total + blocks[k]
    out[0] = total


def join_blocks_kernel(*refs):
    out, at = refs[-1], 0
    for ref in refs[:-1]:
        out[at : at + ref.shape[0]] = ref[...]
        at += ref.shape[0]


def pack_kernel(plan, parts, n_arrays, *refs):
    sources, tables, out, sems = refs[:n_arrays], refs[n_arrays:-2], refs[-2], refs[-1]
    dp_at, chan_at = device_at()
    part = plan.out_own // parts
    rows = pl.ds(pl.multiple_of((dp_at & (parts - 1)) * part, 8), part)
    copies, at = [], 0
    for k, source in enumerate(sources):
        if len(source.shape) == 3:
            copies.append(pltpu.make_async_copy(source.at[:, rows], out.at[at : at + TAPS], sems.at[k]))
            at += TAPS
        else:
            copies.append(pltpu.make_async_copy(source.at[rows], out.at[at], sems.at[k]))
            at += 1
        copies[-1].start()
    if tables:
        narrow, wide = tables[0][...], tables[1][...]
        narrow = jnp.concatenate([narrow, jnp.zeros((4, plan.n_in - plan.in_own), f32)], axis=1)
        narrow = jnp.concatenate([narrow, jnp.zeros((4, plan.n_in), f32)], axis=0)
        wide = jnp.concatenate([wide, jnp.zeros((5, plan.n_out - plan.out_own), f32)], axis=1)
        wide = jnp.concatenate([wide, jnp.zeros((3, plan.n_out), f32)], axis=0)
        narrow = pltpu.roll(narrow, chan_at * plan.in_own, 1)
        wide = pltpu.roll(wide, chan_at * plan.out_own, 1)
        pieces = [narrow[0:4]]
        for k in range(5):
            pieces += [wide[k : k + 1, : plan.n_in], wide[k : k + 1, plan.n_in :]]
        table = jnp.concatenate(pieces + [jnp.zeros((2, plan.n_in), f32)], axis=0)
        for k in range(16 // plan.part):
            out[at + k] = table[k * plan.part : (k + 1) * plan.part]
    wait_all(copies)


def held_sums(plan, recv):
    sums = []
    for which in range(plan.held):
        total = 0.0
        for strip in range(plan.strips):
            total = total + recv[which * plan.strips + gray(strip), :, plan.cells :]
        sums.append(total)
    return sums


def entry_sums_kernel(plan, recv, out):
    for which, total in enumerate(held_sums(plan, recv)):
        out[which] = jnp.concatenate([total, jnp.zeros((plan.in_own, 124), f32)], axis=1)


def own_gain_columns(plan, gains, row):
    _, chan_at = device_at()
    shape = (plan.in_own, plan.n_in)
    own = lax.broadcasted_iota(jnp.int32, shape, 0) + chan_at * plan.in_own
    pick = jnp.where(lax.broadcasted_iota(jnp.int32, shape, 1) == own, gains[row : row + 1], 0.0)
    return jnp.sum(pick, axis=1, keepdims=True)


def input_grad_kernel(plan, dp_masks, group_ref, class_ref, gains, recv, norm, scales, *refs):
    tiles, out = refs[:-1], refs[-1]
    dp_at, chan_at = device_at()
    entries, k = [], 0
    for ref in tiles:
        for block in range(ref.shape[0] // plan.held):
            for which in range(plan.held):
                entries.append(((dp_at ^ dp_masks[k]) * plan.held + which, ref, block * plan.held + which))
            k += 1
    gain_a, gain_b = own_gain_columns(plan, gains, 0), own_gain_columns(plan, gains, 2)
    for which in range(plan.held):
        crop = dp_at * plan.held + which
        count = group_cells(plan, group_ref, class_ref, crop)
        sums = 0.0
        for other, ref, at in entries:
            sums = sums + jnp.where(group_ref[other] == group_ref[crop], 1.0, 0.0).astype(f32) * ref[at]
        sums = sums / count
        shift = sums[:, 0:1] * gain_a + sums[:, 2:3] * gain_b
        slope = sums[:, 1:2] * gain_a + sums[:, 3:4] * gain_b
        pieces = [recv[which * plan.strips + gray(strip), :, : plan.cells] for strip in range(plan.strips)]
        joined = jnp.concatenate(pieces, axis=1)[:, : SIDE * SIDE]
        inside = crop_inside(plan, class_ref, dp_at, which, joined.shape)
        out[which] = scales[which][:, :1] * (joined - shift - norm[which] * slope) * inside


def join_kernel(plan, recv, out):
    for which in range(plan.held):
        pieces = [recv[which * plan.strips + gray(strip)] for strip in range(plan.strips)]
        out[which] = jnp.concatenate(pieces, axis=1)[:, : SIDE * SIDE]


def square_sum(values):
    values = values * values
    while values.ndim > 2:
        values = jnp.sum(values, axis=0)
    return jnp.sum(jnp.sum(values, axis=0, keepdims=True), axis=1, keepdims=True)


def wide_grads_kernel(plan, class_ref, pooled, decoder, middle, style_out, wide_out, squares, turned):
    dp_at, chan_at = device_at()
    vecs, grads, decoder_total, middle_total = [], [], 0.0, 0.0
    for other, mean in enumerate(crop_means(plan, class_ref, pooled)):
        row = unfold(mean)
        vecs.append(row * lax.rsqrt(jnp.sum(row * row, axis=1, keepdims=True) + style_eps))
        sums = crop_sums(plan, decoder, other)
        grads.append(unfold(sums[0:2]))
        decoder_total = decoder_total + sums
        middle_total = middle_total + crop_sums(plan, middle, other)
    blank = -len(vecs) % 8
    if blank:
        vecs.append(jnp.zeros((blank, plan.n_out), f32))
        grads.append(jnp.zeros((blank, plan.n_out), f32))
    vecs, grads = jnp.concatenate(vecs, axis=0), jnp.concatenate(grads, axis=0)
    turned[...] = grads.T
    own = turned[pl.ds(pl.multiple_of(chan_at * plan.out_own, 8), plan.out_own), :]
    style = lax.dot_general(own, vecs, NN, precision=highest, preferred_element_type=f32)
    style_out[...] = style

    first, second = unfold(middle_total[0:2]), unfold(middle_total[2:4])
    third, fourth = unfold(decoder_total[0:2]), unfold(decoder_total[2:4])
    wide = tile([second, first, fourth, third, third], plan.n_out)
    wide = pltpu.roll(wide, (plan.n_out - chan_at * plan.out_own) % plan.n_out, 1)[:5, : plan.out_own]
    wide_out[...] = wide
    squares[...] = jnp.broadcast_to((square_sum(style) + square_sum(wide)) * (1.0 / plan.n_dp), (8, 128))


def narrow_grads_kernel(plan, n_tiles, weights, early, *refs):
    tiles, sums, (narrow_out, squares) = refs[:n_tiles], refs[n_tiles:-2], refs[-2:]
    total = 0.0
    for ref in tiles:
        for at in range(ref.shape[0]):
            total = total + ref[at]
    lanes = jnp.concatenate([total, jnp.zeros((128 - plan.in_own, 128), f32)], axis=0).T
    narrow = jnp.concatenate([lanes[1:2], lanes[0:1], lanes[3:4], lanes[2:3]], axis=0)[:, : plan.in_own]
    narrow_out[...] = narrow
    share = square_sum(narrow) * (1.0 / plan.n_dp)
    for ref, weight in zip(sums, weights):
        share = share + square_sum(ref[0]) * weight
    total = (early[...] + share)[0:1]
    for device in range(squares.shape[0]):
        squares[device] = total


def update_kernel(plan, reductions, senders, counts, *refs):
    squares, refs = refs[: counts[0]], refs[counts[0] :]
    grads = []
    for count in counts[1:]:
        grads.append(refs[:count])
        refs = refs[count:]
    small, refs = refs[:3], refs[3:]
    held, refs = refs[:21], refs[21:]
    outs, norm_out, local, sems = refs[:21], refs[21], refs[22:-1], refs[-1]
    copies = []
    for k in range(21):
        copies.append(pltpu.make_async_copy(held[k], local[k], sems.at[k]))
        copies[-1].start()
    params, moments, seconds = local[:7], local[7:14], local[14:21]
    dp_at, chan_at = device_at()
    total = 0.0
    for device in range(squares[0].shape[0]):
        total = total + squares[0][device]
    norm = jnp.sqrt(total)
    norm_out[...] = jnp.broadcast_to(norm, (8, 128))
    factor = jnp.minimum(1.0, clip_bound / norm[0:1, 0:1])

    rates = (0.06, 0.04, 0.16, 0.04, 1.0, 0.4, 0.4)
    decays = (decay_rate, decay_rate, decay_rate, decay_rate, decay_rate, 0.0, 0.0)
    wait_all(copies)

    def update(which, at, gradient):
        new = adamw(
            params[which][at], gradient * factor, moments[which][at], seconds[which][at], rates[which], decays[which]
        )
        for ref, value in zip(outs[3 * which : 3 * which + 3], new):
            ref[at] = value

    for which, reduction, pieces, masks in zip((0, 1, 3), reductions, grads, senders):
        part = reduction.part
        for ref, mask in zip(pieces, masks):
            rows = pl.ds(pl.multiple_of(((dp_at ^ mask) & (reduction.parts - 1)) * part, 8), part)
            for t in range(TAPS):
                update(which, (t, rows, slice(None)), ref[0, t])
            if which == 1:
                update(2, (rows, slice(None)), ref[0, TAPS, :, : plan.n_in])
    for which, ref in zip((4, 5, 6), small):
        update(which, (slice(None), slice(None)), ref[...])


class Slot:
    def __init__(self, store, at, shape):
        self.store, self.at, self.shape, self.size = store, at, shape, functools.reduce(lambda x, y: x * y, shape)

    def view(self, ref):
        return ref.at[(self.at,) + tuple(slice(0, n) for n in self.shape)]


class Fetched:
    def __init__(self, source, local, sem):
        self.copy, self.local, self.waits = pltpu.make_async_copy(source, local, sem), local, True
        self.shape = local.shape
        self.copy.start()

    def __getitem__(self, at):
        self.wait()
        return self.local[at]

    def wait(self):
        if self.waits:
            self.copy.wait()
        self.waits = False


class Saved:
    def __init__(self, target, local, sem):
        self.target, self.local, self.sem, self.copy = target, local, sem, None

    def __setitem__(self, at, value):
        self.local[...] = value
        self.take(self.local)

    def take(self, ref):
        self.copy = pltpu.make_async_copy(ref, self.target, self.sem)
        self.copy.start()

    def wait(self):
        self.copy.wait()


class Chain:
    def __init__(self, stores):
        self.last, self.cost = None, COST
        self.shapes, self.stores, self.used = stores, {}, {name: 0 for name in stores}

    def slot(self, shape, store="maps"):
        self.used[store] += 1
        return Slot(store, self.used[store] - 1, shape)

    def run(
        self, name, kernel, smem, arrays, out_shapes, scratch=(), flops=0, far=(), more=(), limit=None, passed=None,
        cost=None,
    ):
        cost = self.cost if cost is None else cost
        wanted = [*smem, *arrays, *far, *more]
        spaces = [SMEM] * len(smem) + [VMEM] * len(arrays)
        spaces += [pl.BlockSpec(memory_space=pl.ANY)] * len(far) + [VMEM] * len(more)
        operands = [a for a in wanted if not isinstance(a, Slot)]
        specs = [space for a, space in zip(wanted, spaces) if not isinstance(a, Slot)]
        loads = [a for a in wanted if isinstance(a, Slot)]
        saves = [shape for shape in out_shapes if isinstance(shape, Slot)]
        plain = [shape for shape in out_shapes if not isinstance(shape, Slot)]
        sizes = [functools.reduce(lambda x, y: x * y, shape) for shape in plain]
        small = bool(sizes) and min(sizes) <= 8 * 1024
        shapes = [jax.ShapeDtypeStruct(shape, f32) for shape in plain + ([] if small else [(8, 128)])]
        out_specs, aliases = [VMEM] * len(shapes), {}
        anywhere = pl.BlockSpec(memory_space=pl.ANY)
        rest = [] if self.last is None else [self.last]
        touched = sorted({slot.store for slot in loads + saves})
        for store in touched:
            if store in self.stores:
                rest.append(self.stores[store])
                aliases[len(operands) + len(rest) - 1] = len(shapes)
            shapes.append(jax.ShapeDtypeStruct(self.shapes[store], f32))
            out_specs.append(anywhere)
        if passed is not None:
            rest.append(passed)
            aliases[len(operands) + len(rest) - 1] = len(shapes)
            shapes.append(jax.ShapeDtypeStruct(passed.shape, f32))
            out_specs.append(anywhere)
        moved = 4 * sum(int(a.size) for a in wanted) + 4 * sum(sizes) + 4 * sum(slot.size for slot in saves)
        local = [pltpu.VMEM(slot.shape, f32) for slot in loads + saves]
        if local:
            local.append(pltpu.SemaphoreType.DMA((len(local),)))
        n_plain = len(plain)

        def called(*refs):
            ins, refs = list(refs[: len(operands)]), refs[len(operands) + len(rest) :]
            outs, own, refs = refs[:n_plain], refs[n_plain : len(shapes)], refs[len(shapes) :]
            if not small:
                own[0][...] = jnp.zeros((8, 128), f32)
                own = own[1:]
            stores = dict(zip(touched, own))
            buffers, refs = refs[: len(local)], refs[len(local) :]
            opened = []
            for at, slot in enumerate(loads + saves):
                kind = Fetched if at < len(loads) else Saved
                opened.append(kind(slot.view(stores[slot.store]), buffers[at], buffers[-1].at[at]))
            fetched, saved = iter(opened[: len(loads)]), iter(opened[len(loads) :])
            ins, outs = iter(ins), iter(outs)
            taken = [next(fetched) if isinstance(a, Slot) else next(ins) for a in wanted]
            given = [next(saved) if isinstance(a, Slot) else next(outs) for a in out_shapes]
            kernel(*taken, *given, *refs)
            for one in opened:
                one.wait()

        outs = list(pl.pallas_call(
            called,
            out_shape=shapes,
            in_specs=specs + [anywhere] * len(rest),
            out_specs=out_specs,
            input_output_aliases=aliases,
            scratch_shapes=local + list(scratch),
            cost_estimate=pl.CostEstimate(flops=cost * flops, bytes_accessed=cost * moved, transcendentals=0),
            compiler_params=pltpu.CompilerParams(vmem_limit_bytes=limit or VMEM_LIMIT),
            name=name,
        )(*operands, *rest))
        self.last = outs[sizes.index(min(sizes))] if small else outs[n_plain]
        first = n_plain + (0 if small else 1)
        for k, store in enumerate(touched):
            self.stores[store] = outs[first + k]
        results = iter(outs[:n_plain])
        given = [a if isinstance(a, Slot) else next(results) for a in out_shapes]
        return given if passed is None else given + [outs[-1]]


def adamw(weight, gradient, moment, square, rate, decay):
    first_new = beta_one * moment + (1.0 - beta_one) * gradient
    second_new = beta_two * square + (1.0 - beta_two) * gradient * gradient
    corrected_first = first_new / (1.0 - beta_one**STEP)
    corrected_second = second_new / (1.0 - beta_two**STEP)
    updated = weight - rate * (
        corrected_first / (jnp.sqrt(corrected_second) + adam_eps) + decay * weight
    )
    return (updated, first_new, second_new)


def make_body(mesh):
    def body(
        crop_maps, out_cotangent, norm_group, scale_class,
        entry_conv, middle_conv, shortcut_map, decoder_conv, style_map, narrow_gain_table, wide_gain_table,
        entry_moment, middle_moment, shortcut_moment, decoder_moment, style_moment, narrow_moment, wide_moment,
        entry_square, middle_square, shortcut_square, decoder_square, style_square, narrow_square, wide_square,
    ):
        plan = Plan(mesh, crop_maps.shape, out_cotangent.shape)
        n_in, n_out, n_chan = plan.n_in, plan.n_out, plan.n_chan
        cells, cells_halo = plan.cells, plan.cells_halo
        ids = (norm_group, scale_class)
        weight_shape = (n_chan, plan.parts, TAPS, plan.part, n_out)
        chain = Chain({"maps": (STORED_MAPS, cells_halo, n_out), "weights": (STORED_WEIGHTS,) + weight_shape})
        run, slot = chain.run, chain.slot

        def dp_swap(block, mask):
            return lax.ppermute(block, "dp", [(i, i ^ mask) for i in range(plan.n_dp)])

        def gather_dp(name, block):
            tiles, masks = [block], [0]
            for stage in pair_bits(plan.dp_bits):
                joined = tiles[0] if len(tiles) == 1 else jnp.concatenate(tiles, axis=0)
                with jax.named_scope(name):
                    tiles = [joined] + [dp_swap(joined, mask) for mask in stage]
                masks = masks + [held ^ mask for mask in stage for held in masks]
            return tiles, masks

        def exchange(name, messages):
            everyone, edge_a, edge_b = messages
            with jax.named_scope(name):
                rows = lax.all_to_all(everyone, BOTH, 0, 0)
            if plan.quick:
                with jax.named_scope(name + "_edges"):
                    return rows, swap(edge_a, plan.strip_bits[0], plan), swap(edge_b, plan.strip_bits[1], plan)
            up, down = [], []
            for crop in range(plan.n_crops):
                devices = plan.devices_of(crop)
                down += list(zip(devices[:-1], devices[1:]))
                up += list(zip(devices[1:], devices[:-1]))
            with jax.named_scope(name + "_edges"):
                return rows, lax.ppermute(edge_a, BOTH, down), lax.ppermute(edge_b, BOTH, up)

        by_tap = lambda weight: jnp.transpose(weight, (1, 0, 2))
        n_tables = 16 // plan.part
        stages = pair_bits(plan.chan_bits[:0:-1]) + [[plan.chan_bits[0]]]

        def pack(name, parts, arrays, tables=()):
            taps = sum(TAPS if a.ndim == 3 else 1 for a in arrays) + (n_tables if tables else 0)
            return run(
                name + "_pack", functools.partial(pack_kernel, plan, parts, len(arrays)), (), (),
                [(taps, plan.out_own // parts, arrays[0].shape[-1])], [pltpu.SemaphoreType.DMA((len(arrays),))],
                far=arrays, more=tables,
            )[0]

        class Gathering:
            def __init__(self, name, parts, packed):
                self.name, self.parts = name, parts
                self.block, self.masks, self.left = packed[None], [0], list(stages)
                self.send()

            def send(self):
                stage = self.left.pop(0)
                with jax.named_scope(self.name):
                    self.arrived = [swap(self.block, mask, plan) for mask in stage]
                self.masks = self.masks + [held ^ mask for mask in stage for held in self.masks]

            def join(self):
                joined = [self.block] + self.arrived
                shape = (sum(x.shape[0] for x in joined),) + self.block.shape[1:]
                self.block = run(self.name + "_join", join_blocks_kernel, (), joined, [shape])[0]

            def along_y(self):
                while len(self.left) > 1:
                    self.join()
                    self.send()
                self.join()
                self.send()

            def finish(self, joined):
                if joined:
                    self.join()
                    arrays, senders = [self.block], [(0, self.masks)]
                else:
                    half = len(self.masks) // 2
                    arrays = [self.block] + self.arrived
                    senders = [(0, self.masks[:half]), (0, self.masks[half:])]
                for bit in plan.dp_bits[::-1]:
                    if bit < self.parts:
                        with jax.named_scope(self.name + "_dp"):
                            arrays = arrays + [swap(block, bit * n_chan, plan) for block in arrays]
                        senders = senders + [(dp_mask ^ bit, chans) for dp_mask, chans in senders]
                return Packet(arrays, senders, self.parts)

        packed = pack("wide_weights", plan.parts, (by_tap(middle_conv), by_tap(decoder_conv), style_map))
        with jax.named_scope("wide_weights"):
            gathered = lax.all_gather(packed, "chan")

        maps_shape = crop_maps.shape
        stats = run(
            "entry_stats", functools.partial(stats_kernel, plan), (scale_class,), (crop_maps,),
            [(2, plan.held, plan.in_own, 128)],
        )[0]
        dp_tiles, dp_masks = gather_dp("entry_stats", stats)
        entry_gathering = Gathering(
            "entry_weights", plan.parts,
            pack("entry_weights", plan.parts, (by_tap(entry_conv), shortcut_map), (narrow_gain_table, wide_gain_table)),
        )
        norm_held, scales, send = run(
            "entry_norm", functools.partial(norm_kernel, plan, dp_masks), ids, (crop_maps, *dp_tiles),
            [maps_shape, (plan.held, plan.in_own, 128), (n_chan, plan.in_own, cells_halo)],
        )
        with jax.named_scope("maps"):
            recv = lax.all_to_all(send, "chan", 0, 0).reshape(n_in, cells_halo)
        entry_gathering.along_y()
        narrow = entry_gathering.finish(False)
        top_send = run(
            "pack_top", functools.partial(top_kernel, plan), (scale_class,), (out_cotangent,),
            [(n_chan, plan.out_own, cells_halo)],
        )[0]

        message_shapes = [(plan.n_all, 4, n_out // 2), (SIDE, n_out), (SIDE, n_out)]
        wide_taps, narrow_taps = tap_scratch(plan, n_out), tap_scratch(plan, n_in)
        flat_narrow = pltpu.VMEM((n_out, n_in), f32)
        entry_weight, entry_rest = narrow.scratch(plan, TAPS, n_in), narrow.scratch(plan, 1 + n_tables, n_in)
        flat_wide = pltpu.VMEM((n_out, n_out), f32)
        wide_flops = 2 * 3 * TAPS * cells * n_out * n_out
        narrow_flops = 2 * 3 * TAPS * cells * n_out * n_in

        entry_norm, gains, first_out, shortcut, entry_kept, *messages = run(
            "first_conv", functools.partial(first_kernel, plan, narrow), (scale_class,), (recv,),
            [slot((cells_halo, n_in)), slot((16, n_in)), slot((cells, n_out)), slot((n_out, n_in)),
             slot(weight_shape[:-1] + (n_in,), "weights")] + message_shapes,
            [entry_weight[0], entry_rest[0], entry_weight[1], entry_rest[1]] + narrow_taps, narrow_flops,
            far=narrow.arrays,
        )
        first_stats, edge_a, edge_b = exchange("first_stats", messages)
        top_send = run("top_gate", gate_kernel, (), (first_stats, edge_a, edge_b), [(8, 128)], passed=top_send)[1]
        with jax.named_scope("top"):
            top_recv = lax.all_to_all(top_send, "chan", 0, 0).reshape(n_out, cells_halo)
        gathered = run("wide_weights_gate", gate_kernel, (), (), [(8, 128)], passed=gathered)[1]
        arrays, senders = [gathered], [(0, None)]
        if plan.parts > 1:
            with jax.named_scope("wide_weights_core"):
                arrays, senders = arrays + [swap(gathered, plan.core_mask, plan)], senders + [(1, None)]
        middle, decoder = Packet(arrays, senders, plan.parts), Packet(arrays, senders, plan.parts, TAPS)
        middle_weight = middle.scratch(plan, TAPS, n_out)
        decoder_weight, style_flat = decoder.scratch(plan, TAPS, n_out), decoder.scratch(plan, 1, n_out)

        middle_norm, middle_rows, hidden, middle_kept, *messages = run(
            "second_conv", functools.partial(hidden_kernel, plan, middle), ids,
            (gains, first_out, edge_a, edge_b, entry_norm, first_stats, shortcut),
            [slot((cells_halo, n_out)), slot((8, n_out)), slot((cells, n_out)), slot(weight_shape, "weights")]
            + message_shapes,
            middle_weight + wide_taps, wide_flops, far=middle.arrays,
        )
        hidden_stats, edge_a, edge_b = exchange("hidden_stats", messages)

        top_halo, top_back, style, decoder_kept = run(
            "top_back", functools.partial(top_back_kernel, plan, decoder), (), (top_recv,),
            [slot((cells_halo, n_out)), slot((cells, n_out)), slot((n_out, n_out)), slot(weight_shape, "weights")],
            [decoder_weight[0], style_flat[0], decoder_weight[1], style_flat[1]] + wide_taps, wide_flops,
            far=decoder.arrays, cost=HIDE,
        )

        decoder_norm, decoder_rows, decoder_pre_grad, *messages = run(
            "decoder_norm", functools.partial(decoder_kernel, plan), ids,
            (gains, hidden, edge_a, edge_b, top_back, hidden_stats, style),
            [slot((cells_halo, n_out)), slot((8, n_out)), slot((cells, n_out))] + message_shapes,
        )
        decoder_sums, edge_a, edge_b = exchange("decoder_sums", messages)

        def add(name, left, right, count):
            shape = (left.shape[0] // count,) + left.shape[1:]
            return run(name + "_add", functools.partial(add_kernel, count), (), (left, right), [shape] * count)

        def sum_cores(name, halves, count):
            keep, away = halves
            if plan.parts == 1:
                return [keep[k * keep.shape[0] // count : (k + 1) * keep.shape[0] // count] for k in range(count)]
            with jax.named_scope(name + "_core"):
                arrived = swap(away, plan.core_mask, plan)
            return add(name, keep, arrived, count)

        def sum_far(name, total, reduction):
            for bit in plan.dp_bits:
                if bit >= reduction.parts:
                    with jax.named_scope(name + "_far"):
                        arrived = swap(total, bit * n_chan, plan)
                    total = run(name + "_total", total_kernel, (), (total, arrived), [total.shape])[0]
            return total

        def all_parts(name, total, reduction):
            pieces, masks = [total], [0]
            for bit in plan.dp_bits[::-1]:
                if bit < reduction.parts:
                    with jax.named_scope(name + "_back"):
                        pieces = pieces + [swap(piece, bit * n_chan, plan) for piece in pieces]
                    masks = masks + [mask ^ bit for mask in masks]
            return pieces, masks

        def halve(name, pair, bit, last):
            with jax.named_scope(name + "_half"):
                arrived = swap(pair[1], bit, plan)
            return add(name, pair[0], arrived, pair[0].shape[0] if last else 2)

        def collect(name, blocks, reduction):
            with jax.named_scope(name + "_last"):
                arrived = [swap(b, mask, plan) for b, mask in zip(blocks[1:], reduction.last[1:])]
            return run(name + "_total", total_kernel, (), (blocks[0], *arrived), [blocks[0].shape])[0]

        decoder_plan = Reduction(plan, TAPS, plan.parts)
        cross = [2 * n_chan] if plan.wide_parts > 2 else []
        middle_plan = Reduction(plan, TAPS + 1, plan.wide_parts, cross + plan.chan_bits[:1])
        entry_plan = Reduction(plan, TAPS, plan.parts, plan.chan_bits[:1])

        decoder_halves = run(
            "decoder_wgrad", functools.partial(decoder_weight_kernel, plan, decoder_plan), (scale_class,),
            (gains, top_halo, decoder_norm, decoder_rows), [decoder_plan.shape(n_out)] * 2,
            [flat_wide] + wide_taps, wide_flops, cost=HIDE,
        )
        out_send = run(
            "decoder_conv", functools.partial(out_kernel, plan), (scale_class,),
            (gains, hidden, decoder_norm, decoder_rows, decoder_kept),
            [(n_chan, plan.out_own, cells)], wide_taps, wide_flops, cost=HIDE,
        )[0]

        hidden_grad, middle_pre_grad, *messages = run(
            "second_back", functools.partial(hidden_back_kernel, plan), ids,
            (gains, decoder_pre_grad, edge_a, edge_b, decoder_norm, decoder_rows, top_halo, middle_norm,
             decoder_sums, style, middle_kept),
            [slot((cells_halo, n_out)), slot((cells, n_out))] + message_shapes,
            wide_taps, wide_flops,
        )
        middle_sums, edge_a, edge_b = exchange("middle_sums", messages)
        chain.cost = MIDDLE
        decoder_half = sum_cores("decoder_grads", decoder_halves, 1)[0]
        with jax.named_scope("decoder_grads_scatter"):
            decoder_grads = lax.psum_scatter(decoder_half, "chan", scatter_dimension=0, tiled=True)
        shortcut_grad, *middle_halves = run(
            "middle_wgrad", functools.partial(middle_weight_kernel, plan, middle_plan), (scale_class,),
            (gains, hidden_grad, middle_norm, entry_norm, shortcut),
            [slot((cells, n_in))] + [middle_plan.shape(n_out)] * 2,
            [flat_wide] + wide_taps, wide_flops, cost=MIDDLE,
        )
        out_send = run("block_gate", gate_kernel, (), (middle_sums, edge_a, edge_b), [(8, 128)], passed=out_send)[1]
        with jax.named_scope("block_out"):
            out_recv = lax.all_to_all(out_send, "chan", 0, 0)

        chain.cost = TAIL
        first_grad, *halves = run(
            "first_grad", functools.partial(first_grad_kernel, plan, entry_plan), ids,
            (gains, middle_pre_grad, edge_a, edge_b, middle_norm, middle_rows, entry_norm, middle_sums),
            [slot((cells_halo, n_out))] + [entry_plan.shape(n_in)] * 2, [flat_narrow] + narrow_taps, narrow_flops,
        )

        entry_pair = sum_cores("entry_grads", halves, 2)
        middle_pair = sum_cores("middle_grads", middle_halves, 2)
        block_out = run(
            "block_out", functools.partial(join_kernel, plan), (), (out_recv,), [out_cotangent.shape], cost=HIDE
        )[0]
        entry_blocks = halve("entry_grads", entry_pair, plan.chan_bits[0], True)
        send = run(
            "first_back", functools.partial(first_back_kernel, plan), (scale_class,),
            (gains, first_grad, entry_norm, shortcut_grad, entry_kept),
            [(n_chan, plan.in_own, cells + 4)], wide_taps, narrow_flops,
        )[0]
        with jax.named_scope("input_grad"):
            recv = lax.all_to_all(send, "chan", 0, 0)
        for k, bit in enumerate(middle_plan.halving[:-1]):
            middle_pair = halve("middle_grads", middle_pair, bit, False)
        style_sum, wide_sum, early_share = run(
            "wide_grads", functools.partial(wide_grads_kernel, plan), (scale_class,),
            (hidden_stats, decoder_sums, middle_sums), [(plan.out_own, n_out), (5, plan.out_own), (8, 128)],
            [pltpu.VMEM((n_out, -(-plan.n_crops // 8) * 8), f32)],
        )
        entry_sums = run(
            "entry_sums", functools.partial(entry_sums_kernel, plan), (), (recv,), [(plan.held, plan.in_own, 128)]
        )[0]
        entry_tiles, entry_masks = gather_dp("entry_sums", entry_sums)
        entry_total = collect("entry_grads", entry_blocks, entry_plan)
        middle_blocks = halve("middle_grads", middle_pair, middle_plan.halving[-1], True)
        entry_total = sum_far("entry_grads", entry_total, entry_plan)
        input_grad = run(
            "input_grad", functools.partial(input_grad_kernel, plan, entry_masks), ids,
            (gains, recv, norm_held, scales, *entry_tiles), [maps_shape],
        )[0]
        middle_total = collect("middle_grads", middle_blocks, middle_plan)
        middle_total = sum_far("middle_grads", middle_total, middle_plan)
        decoder_total = sum_far("decoder_grads", decoder_grads, decoder_plan)
        totals, plans = [entry_total, middle_total, decoder_total], [entry_plan, middle_plan, decoder_plan]
        names = ("entry_grads", "middle_grads", "decoder_grads")
        parted = [all_parts(name, total, held) for name, total, held in zip(names, totals, plans)]
        pieces, senders = [p for p, _ in parted], [m for _, m in parted]
        narrow_sum, squares = run(
            "narrow_grads", functools.partial(narrow_grads_kernel, plan, len(entry_tiles), [p.parts / plan.n_dp for p in plans]), (),
            (early_share, *entry_tiles, *totals), [(4, plan.in_own), (plan.n_all, 1, 128)],
        )
        with jax.named_scope("norm"):
            tiles = [lax.all_to_all(squares, BOTH, 0, 0)]
        params = (entry_conv, middle_conv, shortcut_map, decoder_conv, style_map, narrow_gain_table, wide_gain_table)
        moments = (
            entry_moment, middle_moment, shortcut_moment, decoder_moment, style_moment, narrow_moment, wide_moment,
        )
        seconds = (
            entry_square, middle_square, shortcut_square, decoder_square, style_square, narrow_square, wide_square,
        )
        turned = [by_tap(a) if a.ndim == 3 else a for a in params + moments + seconds]
        counts = [len(tiles)] + [len(p) for p in pieces]
        *updated, norm = run(
            "update", functools.partial(update_kernel, plan, plans, senders, counts), (),
            (*tiles, *[p for held in pieces for p in held], style_sum, narrow_sum, wide_sum),
            [p.shape for p in turned[:7] for _ in range(3)] + [(8, 128)],
            [pltpu.VMEM(p.shape, f32) for p in turned] + [pltpu.SemaphoreType.DMA((21,))],
            far=turned, limit=60 * 2**20,
        )
        updated = [by_tap(a) if a.ndim == 3 else a for a in updated]
        return (block_out, input_grad, *updated, norm[0, 0])

    return body


def solution(mesh):
    maps, whole = P("dp", "chan", None), P()
    conv_spec, flat_spec, table_spec = P("chan", None, None), P("chan", None), P(None, "chan")
    params = (conv_spec, conv_spec, flat_spec, conv_spec, flat_spec, table_spec, table_spec)
    updated = tuple(spec for spec in params for _ in range(3))
    return jax.shard_map(
        make_body(mesh),
        mesh=mesh,
        in_specs=(maps, maps, whole, whole) + params * 3,
        out_specs=(maps, maps) + updated + (whole,),
        check_vma=False,
    )
```

```python
import functools

import jax
import jax.numpy as jnp
from jax import lax
from jax.experimental import pallas as pl
from jax.experimental.pallas import tpu as pltpu
from jax.sharding import PartitionSpec as P

SIDE = 56
H_SMALL = 40
NGRP = 4
STEP = 10
TAPS = 9
VMEM_LIMIT = 20 * 2**20
COST = 1
TAIL = 1
STORED_MAPS, STORED_WEIGHTS = 60, 22
HIDE = 1
MIDDLE = 0

beta_one = 0.9
beta_two = 0.999
adam_eps = 1e-08
decay_rate = 0.01
clip_bound = 1.0
norm_eps = 1e-05
style_eps = 1e-06
highest = lax.Precision.HIGHEST
BOTH = ("dp", "chan")
f32, bf16 = jnp.float32, jnp.bfloat16
SMEM = pl.BlockSpec(memory_space=pltpu.SMEM)
VMEM = pl.BlockSpec(memory_space=pltpu.VMEM)
NN = (((1,), (0,)), ((), ()))
NT = (((1,), (1,)), ((), ()))


def gray(number):
    return number ^ (number >> 1)


def pair_bits(bits):
    stages = []
    for start in range(0, len(bits), 2):
        pair = bits[start : start + 2]
        stages.append([pair[0]] if len(pair) == 1 else [pair[0], pair[1], pair[0] ^ pair[1]])
    return stages


class Plan:
    def __init__(self, mesh, crop_shape, out_shape):
        self.n_dp, self.n_chan = mesh.shape["dp"], mesh.shape["chan"]
        self.n_all = self.n_dp * self.n_chan
        self.held, self.in_own = crop_shape[0], crop_shape[1]
        self.out_own = out_shape[1]
        self.n_in, self.n_out = self.in_own * self.n_chan, self.out_own * self.n_chan
        self.n_crops = self.held * self.n_dp
        self.strips = self.n_chan // self.held
        self.rows = -(-SIDE // self.strips)
        self.cells, self.cells_halo = self.rows * SIDE, (self.rows + 2) * SIDE
        self.strip_of = [0] * self.strips
        for strip in range(self.strips):
            self.strip_of[gray(strip)] = strip
        self.parts = 2 if self.out_own % 16 == 0 and self.n_dp >= 2 else 1
        self.part = self.out_own // self.parts
        self.wide_parts = 4 if self.out_own % 32 == 0 and self.n_dp >= 4 else self.parts
        self.core_mask = self.n_chan
        self.strip_bits = [1 << k for k in range(self.strips.bit_length() - 1)]
        self.chan_bits = [1 << k for k in range(self.n_chan.bit_length() - 1)]
        self.crop_bits = [1 << k for k in range(self.n_chan.bit_length() - 1) if (1 << k) >= self.strips]
        self.far_bits = [self.n_chan << k for k in range(1, self.n_dp.bit_length() - 1)]
        self.dp_bits = [1 << k for k in range(self.n_dp.bit_length() - 1)]
        self.quick = self.strips == 4

    def devices_of(self, crop):
        base = crop // self.held * self.n_chan + crop % self.held * self.strips
        return [base + gray(strip) for strip in range(self.strips)]


def swap(block, mask, plan):
    return lax.ppermute(block, BOTH, [(i, i ^ mask) for i in range(plan.n_all)])


def split(values):
    top = values.astype(bf16)
    return top, (values - top.astype(f32)).astype(bf16)


def dot3(left, right, dims):
    (left_top, left_low), (right_top, right_low) = left, right
    dot = functools.partial(lax.dot_general, dimension_numbers=dims, preferred_element_type=f32)
    return dot(left_top, right_top) + dot(left_low, right_top) + dot(left_top, right_low)


def device_at():
    return lax.axis_index("dp"), lax.axis_index("chan")


def crop_strip(plan, dp_at, chan_at):
    low = chan_at & (plan.strips - 1)
    strip = low
    for k in range(1, plan.strips.bit_length() - 1):
        strip = strip ^ (low >> k)
    return dp_at * plan.held + chan_at // plan.strips, strip


def side_of(class_ref, crop):
    return jnp.where(class_ref[crop] == 0, SIDE, H_SMALL)


def group_cells(plan, group_ref, class_ref, crop):
    total = jnp.int32(0)
    for other in range(plan.n_crops):
        side = side_of(class_ref, other)
        total = total + jnp.where(group_ref[other] == group_ref[crop], side * side, 0)
    return total.astype(f32)


def inside_mask(plan, class_ref, crop, strip, columns, halo):
    side = side_of(class_ref, crop)
    col = lax.broadcasted_iota(jnp.int32, (SIDE, columns), 0)
    in_cols = jnp.where(col < side, 1.0, 0.0).astype(f32)
    rows = range(-1, plan.rows + 1) if halo else range(plan.rows)
    pieces = []
    for row in rows:
        at = strip * plan.rows + row
        pieces.append(in_cols * jnp.where((at >= 0) & (at < side), 1.0, 0.0).astype(f32))
    return jnp.concatenate(pieces, axis=0)


def shifted_columns(values):
    length = values.shape[0]
    col = lax.broadcasted_iota(jnp.int32, values.shape, 0) % SIDE
    left = jnp.where(col == 0, 0.0, jnp.roll(values, 1, 0))
    right = jnp.where(col == SIDE - 1, 0.0, jnp.roll(values, -1, 0))
    return left, values, right


def fill_taps(plan, values, even, odd):
    for b, moved in enumerate(shifted_columns(values)):
        top, low = split(moved)
        even[0, b], even[1, b] = top, low
        top, low = split(moved[SIDE : SIDE + plan.cells])
        odd[0, b], odd[1, b] = top, low


def read_tap(plan, even, odd, a, b):
    if a == 1:
        return odd[0, b], odd[1, b]
    start = 2 * SIDE if a == 2 else 0
    return even[0, b, start : start + plan.cells], even[1, b, start : start + plan.cells]


def tap_scratch(plan, columns):
    return [
        pltpu.VMEM((2, 3, plan.cells_halo, columns), bf16),
        pltpu.VMEM((2, 3, plan.cells, columns), bf16),
    ]


class Packet:
    def __init__(self, arrays, senders, parts, base=0):
        self.arrays, self.senders, self.parts, self.base = arrays, senders, parts, base

    def scratch(self, plan, taps, columns):
        n, part = sum(len(chans or [0]) for _, chans in self.senders), plan.out_own // self.parts
        return [
            pltpu.VMEM((plan.n_chan, self.parts, taps, part, columns), f32), pltpu.SemaphoreType.DMA((n,))
        ]

    def load(self, plan, refs, first, taps, weight, sems):
        dp_at, chan_at = device_at()
        copies, first = [], first + self.base
        for ref, (dp_mask, chans) in zip(refs, self.senders):
            place = (dp_at ^ dp_mask) & (self.parts - 1)
            if chans is None:
                pairs = [(ref.at[:, first : first + taps], weight.at[:, place])]
            else:
                pairs = [
                    (ref.at[j, first : first + taps], weight.at[chan_at ^ mask, place])
                    for j, mask in enumerate(chans)
                ]
            for source, target in pairs:
                copy = pltpu.make_async_copy(source, target, sems.at[len(copies)])
                copy.start()
                copies.append(copy)
        return copies


def wait_all(copies):
    for copy in copies:
        copy.wait()


def tap_weight(weight, t):
    block = weight[:, :, t]
    return block.reshape(block.shape[0] * block.shape[1] * block.shape[2], block.shape[3])


def conv_forward(plan, even, odd, weight):
    total = None
    for a in range(3):
        for b in range(3):
            term = dot3(read_tap(plan, even, odd, a, b), split(tap_weight(weight, 3 * a + b)), NT)
            total = term if total is None else total + term
    return total


def conv_backward(plan, even, odd, weight):
    total = None
    for a in range(3):
        for b in range(3):
            term = dot3(read_tap(plan, even, odd, 2 - a, 2 - b), split(tap_weight(weight, 3 * a + b)), NN)
            total = term if total is None else total + term
    return total


def row_sum(values):
    return jnp.sum(values, axis=0, keepdims=True)


def tile(rows, columns):
    blank = jnp.zeros((8 - len(rows), columns), f32)
    return jnp.concatenate(list(rows) + [blank], axis=0)


def fold(row):
    half = row.shape[1] // 2
    return jnp.concatenate([row[:, :half], row[:, half:]], axis=0)


def unfold(pair):
    return jnp.concatenate([pair[0:1], pair[1:2]], axis=1)


def strip_cells(plan, side, strip):
    return (jnp.clip(side - strip * plan.rows, 0, plan.rows) * side).astype(f32)


def local_stats(plan, class_ref, crop, strip, values, inside):
    mean = row_sum(values * inside) / jnp.maximum(strip_cells(plan, side_of(class_ref, crop), strip), 1.0)
    centered = (values - mean) * inside
    return mean, row_sum(centered * centered)


def write_messages(plan, strip, rows, values, messages):
    everyone, edge_a, edge_b = messages
    block = jnp.concatenate([fold(row) for row in rows], axis=0)
    for device in range(plan.n_all):
        everyone[device] = block
    first, last = values[:SIDE], values[-SIDE:]
    edge_a[...] = jnp.where((strip & 1) == 0, last, first) if plan.quick else last
    edge_b[...] = jnp.where(strip == 1, last, first) if plan.quick else first


def with_edges(plan, strip, values, edge_a, edge_b):
    a, b = edge_a[...], edge_b[...]
    if plan.quick:
        a_above = (strip & 1) == 1
        above, below = jnp.where(a_above, a, b), jnp.where(a_above, b, a)
    else:
        above, below = a, b
    return jnp.concatenate([above, values, below], axis=0)


def same_group(group_ref, other, crop):
    return jnp.where(group_ref[other] == group_ref[crop], 1.0, 0.0).astype(f32)


def crop_means(plan, class_ref, stats):
    means = []
    for other in range(plan.n_crops):
        side = side_of(class_ref, other)
        mean = 0.0
        for strip, device in enumerate(plan.devices_of(other)):
            mean = mean + strip_cells(plan, side, strip) * stats[device, 0:2]
        means.append(mean / (side * side).astype(f32))
    return means


def group_stats(plan, group_ref, class_ref, crop, stats):
    count = group_cells(plan, group_ref, class_ref, crop)
    weights, mean = [], 0.0
    for other in range(plan.n_crops):
        same, side = same_group(group_ref, other, crop), side_of(class_ref, other)
        for strip, device in enumerate(plan.devices_of(other)):
            weights.append((device, same, same * strip_cells(plan, side, strip)))
            mean = mean + weights[-1][2] * stats[device, 0:2]
    mean = mean / count
    total = 0.0
    for device, same, cells in weights:
        spread = stats[device, 0:2] - mean
        total = total + same * stats[device, 2:4] + cells * (spread * spread)
    return unfold(mean), unfold(lax.rsqrt(total / count + norm_eps))


def crop_sums(plan, sums, other):
    total = 0.0
    for device in plan.devices_of(other):
        total = total + sums[device]
    return total


def group_sums(plan, group_ref, crop, sums):
    total = 0.0
    for other in range(plan.n_crops):
        total = total + same_group(group_ref, other, crop) * crop_sums(plan, sums, other)
    return unfold(total[0:2]), unfold(total[2:4])


def own_crop(plan, crop, pairs):
    total = 0.0
    for other, pair in enumerate(pairs):
        total = total + jnp.where(crop == other, pair, 0.0)
    return unfold(total)


def sigmoid(values):
    return 1.0 / (1.0 + jnp.exp(-values))


def silu(values):
    return values * sigmoid(values)


def silu_slope(values):
    sig = sigmoid(values)
    return sig * (1.0 + values * (1.0 - sig))


def crop_inside(plan, class_ref, dp_at, which, shape):
    side = side_of(class_ref, dp_at * plan.held + which)
    at = lax.broadcasted_iota(jnp.int32, shape, 1)
    row = at // SIDE
    return jnp.where((row < side) & (at - row * SIDE < side), 1.0, 0.0).astype(f32)


def stats_kernel(plan, class_ref, maps, out):
    dp_at, _ = device_at()
    for which in range(plan.held):
        inside = crop_inside(plan, class_ref, dp_at, which, maps.shape[1:])
        side = side_of(class_ref, dp_at * plan.held + which)
        cells = (side * side).astype(f32)
        values = maps[which] * inside
        mean = jnp.sum(values, axis=1, keepdims=True) / cells
        centered = (values - mean) * inside
        squares = jnp.sum(centered * centered, axis=1, keepdims=True)
        out[0, which] = jnp.broadcast_to(mean, (plan.in_own, 128))
        out[1, which] = jnp.broadcast_to(squares, (plan.in_own, 128))


def pack_strips(plan, values, which, send):
    blank = jnp.zeros((values.shape[0], SIDE), f32)
    tail = plan.strips * plan.rows - SIDE + 1
    padded = jnp.concatenate([blank, values] + [blank] * tail, axis=1)
    for strip in range(plan.strips):
        first = strip * plan.cells
        send[which * plan.strips + gray(strip)] = padded[:, first : first + plan.cells_halo]


def norm_kernel(plan, masks, group_ref, class_ref, maps, *refs):
    parts, (norm, scales, send) = refs[:-3], refs[-3:]
    dp_at, _ = device_at()
    entries, k = [], 0
    for ref in parts:
        for block in range(ref.shape[0] // 2):
            for which in range(plan.held):
                entries.append(((dp_at ^ masks[k]) * plan.held + which, ref, block, which))
            k += 1
    for which in range(plan.held):
        crop = dp_at * plan.held + which
        count = group_cells(plan, group_ref, class_ref, crop)
        mean, total = 0.0, 0.0
        for other, ref, block, held in entries:
            side = side_of(class_ref, other)
            weight = jnp.where(group_ref[other] == group_ref[crop], side * side, 0).astype(f32)
            mean = mean + weight * ref[2 * block, held]
        mean = mean / count
        for other, ref, block, held in entries:
            side = side_of(class_ref, other)
            same = group_ref[other] == group_ref[crop]
            spread = ref[2 * block, held] - mean
            total = total + jnp.where(same, 1.0, 0.0).astype(f32) * ref[2 * block + 1, held]
            total = total + jnp.where(same, side * side, 0).astype(f32) * (spread * spread)
        scale = lax.rsqrt(total / count + norm_eps)
        scales[which] = scale
        inside = crop_inside(plan, class_ref, dp_at, which, maps.shape[1:])
        values = (maps[which] * inside - mean[:, :1]) * inside * scale[:, :1]
        norm[which] = values
        pack_strips(plan, values, which, send)


def gate_kernel(*refs):
    refs[-1][...] = jnp.zeros((8, 128), f32)


def top_kernel(plan, class_ref, top, send):
    dp_at, _ = device_at()
    for which in range(plan.held):
        inside = crop_inside(plan, class_ref, dp_at, which, top.shape[1:])
        pack_strips(plan, top[which] * inside, which, send)


def first_kernel(plan, packet, class_ref, recv, *refs):
    n = len(packet.arrays)
    packets, refs = refs[:n], refs[n:]
    entry_norm, gains, first_out, shortcut, kept, everyone, edge_a, edge_b = refs[:8]
    weight, rest, sems, rest_sems, even, odd = refs[8:]
    n_tables = 16 // plan.part
    copies = packet.load(plan, packets, 0, TAPS, weight, sems)
    rest_copies = packet.load(plan, packets, TAPS, 1 + n_tables, rest, rest_sems)
    dp_at, chan_at = device_at()
    crop, strip = crop_strip(plan, dp_at, chan_at)
    norm = recv[...].T
    entry_norm[...] = norm
    inside = inside_mask(plan, class_ref, crop, strip, plan.n_in, True)
    wait_all(rest_copies)
    table = 0.0
    for j in range(plan.n_chan):
        table = table + jnp.concatenate([rest[j, 0, 1 + k] for k in range(n_tables)], axis=0)
    gains[...] = table
    shortcut[...] = tap_weight(rest, 0)
    pre = norm * table[0:1] + table[1:2]
    fill_taps(plan, silu(pre) * inside, even, odd)
    wait_all(copies)
    kept.take(weight)
    out = conv_forward(plan, even, odd, weight)
    first_out[...] = out
    inside = inside_mask(plan, class_ref, crop, strip, plan.n_out, False)
    stats = local_stats(plan, class_ref, crop, strip, out, inside)
    write_messages(plan, strip, stats, out, (everyone, edge_a, edge_b))


def wide_rows(gains):
    return [jnp.concatenate([gains[4 + 2 * k : 5 + 2 * k], gains[5 + 2 * k : 6 + 2 * k]], axis=1) for k in range(5)]


def hidden_kernel(
    plan, packet, group_ref, class_ref, gains, first_out, edge_a, edge_b, entry_norm, stats, shortcut, *refs
):
    n = len(packet.arrays)
    packets, refs = refs[:n], refs[n:]
    middle_norm, norm_rows, hidden, kept, everyone, with_a, with_b, weight, sems, even, odd = refs
    copies = packet.load(plan, packets, 0, TAPS, weight, sems)
    dp_at, chan_at = device_at()
    crop, strip = crop_strip(plan, dp_at, chan_at)
    wide = wide_rows(gains)
    mean, scale = group_stats(plan, group_ref, class_ref, crop, stats)
    norm_rows[...] = tile([mean, scale], plan.n_out)
    inside = inside_mask(plan, class_ref, crop, strip, plan.n_out, True)
    norm = (with_edges(plan, strip, first_out[...], edge_a, edge_b) - mean) * inside * scale
    middle_norm[...] = norm
    fill_taps(plan, silu(norm * wide[0] + wide[1]) * inside, even, odd)
    inside = inside[SIDE : SIDE + plan.cells]
    shortcut_in = (entry_norm[SIDE : SIDE + plan.cells] * gains[2:3] + gains[3:4]) * inside[:, : plan.n_in]
    out = dot3(split(shortcut_in), split(shortcut[...]), NT)
    wait_all(copies)
    kept.take(weight)
    out = (conv_forward(plan, even, odd, weight) + out) * inside
    hidden[...] = out
    stats = local_stats(plan, class_ref, crop, strip, out, inside)
    write_messages(plan, strip, stats, out, (everyone, with_a, with_b))


def top_back_kernel(plan, packet, recv, *refs):
    n = len(packet.arrays)
    packets, (top_halo, out, style, kept, weight, flat, sems, flat_sems, even, odd) = refs[:n], refs[n:]
    copies = packet.load(plan, packets, 0, TAPS, weight, sems)
    flat_copies = packet.load(plan, packets, TAPS, 1, flat, flat_sems)
    top = recv[...].T
    top_halo[...] = top
    fill_taps(plan, top, even, odd)
    wait_all(flat_copies)
    style[...] = tap_weight(flat, 0)
    wait_all(copies)
    kept.take(weight)
    out[...] = conv_backward(plan, even, odd, weight)


def decoder_kernel(plan, group_ref, class_ref, gains, hidden, edge_a, edge_b, top_back, stats, style, *refs):
    decoder_norm, norm_rows, pre_grad, alone, with_a, with_b = refs
    dp_at, chan_at = device_at()
    crop, strip = crop_strip(plan, dp_at, chan_at)
    wide = wide_rows(gains)
    mean, scale = group_stats(plan, group_ref, class_ref, crop, stats)
    pooled = own_crop(plan, crop, crop_means(plan, class_ref, stats))
    style_scale = lax.rsqrt(jnp.sum(pooled * pooled, axis=1, keepdims=True) + style_eps)
    style_vec = pooled * style_scale
    eight = jnp.broadcast_to(style_vec, (8, plan.n_out))
    term = lax.dot_general(eight, style[...], NT, precision=highest, preferred_element_type=f32)[0:1]
    shift = wide[3] + (term + wide[4])
    norm_rows[...] = tile(
        [mean, scale, shift, style_vec, jnp.broadcast_to(style_scale, (1, plan.n_out))], plan.n_out
    )
    inside = inside_mask(plan, class_ref, crop, strip, plan.n_out, True)
    norm = (with_edges(plan, strip, hidden[...], edge_a, edge_b) - mean) * inside * scale
    decoder_norm[...] = norm
    own = norm[SIDE : SIDE + plan.cells]
    grad = top_back[...] * silu_slope(own * wide[2] + shift) * inside[SIDE : SIDE + plan.cells]
    pre_grad[...] = grad
    write_messages(plan, strip, (row_sum(grad), row_sum(grad * own)), grad, (alone, with_a, with_b))


def out_kernel(plan, class_ref, gains, hidden, decoder_norm, norm_rows, weight, send, even, odd):
    dp_at, chan_at = device_at()
    crop, strip = crop_strip(plan, dp_at, chan_at)
    wide = wide_rows(gains)
    inside = inside_mask(plan, class_ref, crop, strip, plan.n_out, True)
    fill_taps(plan, silu(decoder_norm[...] * wide[2] + norm_rows[2:3]) * inside, even, odd)
    out = hidden[...] + conv_forward(plan, even, odd, weight) * inside[SIDE : SIDE + plan.cells]
    out = out.T
    for chan in range(plan.n_chan):
        send[chan] = out[chan * plan.out_own : (chan + 1) * plan.out_own]


def hidden_back_kernel(
    plan, group_ref, class_ref, gains, pre_grad, edge_a, edge_b,
    decoder_norm, norm_rows, top_halo, middle_norm, all_sums, style, weight, *refs
):
    hidden_grad, out, alone, with_a, with_b, even, odd = refs
    dp_at, chan_at = device_at()
    crop, strip = crop_strip(plan, dp_at, chan_at)
    wide = wide_rows(gains)
    shift, slope = group_sums(plan, group_ref, crop, all_sums)
    count = group_cells(plan, group_ref, class_ref, crop)
    style_vec, style_scale = norm_rows[3:4], norm_rows[4:5]
    own_grad = own_crop(plan, crop, [crop_sums(plan, all_sums, other)[0:2] for other in range(plan.n_crops)])
    eight = jnp.broadcast_to(own_grad, (8, plan.n_out))
    vec_grad = lax.dot_general(eight, style[...], NN, precision=highest, preferred_element_type=f32)[0:1]
    pooled_grad = style_scale * (vec_grad - style_vec * jnp.sum(vec_grad * style_vec, axis=1, keepdims=True))
    side = side_of(class_ref, crop)
    pooled_grad = pooled_grad / (side * side).astype(f32)
    grad = with_edges(plan, strip, pre_grad[...], edge_a, edge_b)
    inside = inside_mask(plan, class_ref, crop, strip, plan.n_out, True)
    grad = norm_rows[1:2] * wide[2] * (grad - shift / count - decoder_norm[...] * (slope / count))
    grad = top_halo[...] + (grad + pooled_grad) * inside
    hidden_grad[...] = grad
    fill_taps(plan, grad, even, odd)
    own = middle_norm[SIDE : SIDE + plan.cells]
    result = conv_backward(plan, even, odd, weight) * silu_slope(own * wide[0] + wide[1])
    result = result * inside[SIDE : SIDE + plan.cells]
    out[...] = result
    write_messages(plan, strip, (row_sum(result), row_sum(result * own)), result, (alone, with_a, with_b))


def first_grad_kernel(
    plan, reduction, group_ref, class_ref, gains, pre_grad, edge_a, edge_b,
    middle_norm, norm_rows, entry_norm, all_sums, *refs
):
    first_grad, keep, away, result, even, odd = refs
    dp_at, chan_at = device_at()
    crop, strip = crop_strip(plan, dp_at, chan_at)
    wide = wide_rows(gains)
    shift, slope = group_sums(plan, group_ref, crop, all_sums)
    count = group_cells(plan, group_ref, class_ref, crop)
    grad = with_edges(plan, strip, pre_grad[...], edge_a, edge_b)
    inside = inside_mask(plan, class_ref, crop, strip, plan.n_out, True)
    grad = norm_rows[1:2] * wide[0] * (grad - shift / count - middle_norm[...] * (slope / count)) * inside
    first_grad[...] = grad
    act = silu(entry_norm[...] * gains[0:1] + gains[1:2]) * inside[:, : plan.n_in]
    fill_taps(plan, act, even, odd)
    weight_grad(plan, reduction, grad[SIDE : SIDE + plan.cells], even, odd, keep, away, result)


def first_back_kernel(
    plan, class_ref, gains, first_grad, entry_norm, shortcut_grad, weight, send, even, odd
):
    dp_at, chan_at = device_at()
    crop, strip = crop_strip(plan, dp_at, chan_at)
    fill_taps(plan, first_grad[...], even, odd)
    own = entry_norm[SIDE : SIDE + plan.cells]
    result = conv_backward(plan, even, odd, weight) * silu_slope(own * gains[0:1] + gains[1:2])
    result = result * inside_mask(plan, class_ref, crop, strip, plan.n_in, False)
    other = shortcut_grad[...]
    sums = tile([row_sum(result), row_sum(result * own), row_sum(other), row_sum(other * own)], plan.n_in).T
    joined = (result * gains[0:1] + other * gains[2:3]).T
    for chan in range(plan.n_chan):
        rows = slice(chan * plan.in_own, (chan + 1) * plan.in_own)
        send[chan, :, : plan.cells] = joined[rows]
        send[chan, :, plan.cells :] = sums[rows, :4]


class Reduction:
    def __init__(self, plan, taps, parts, halving=None):
        self.taps, self.parts, self.part = taps, parts, plan.out_own // parts
        self.halving, self.masks, self.blocks = halving, None, plan.n_chan
        if halving is None:
            return
        self.last = [0]
        for bit in plan.chan_bits:
            if bit not in halving:
                self.last = self.last + [mask | bit for mask in self.last]
        self.masks = self.last
        for bit in halving[::-1]:
            self.masks = self.masks + [mask | bit for mask in self.masks]
        self.blocks = len(self.masks)

    def shape(self, columns):
        return (self.blocks, self.taps, self.part, columns)


def place_rows(plan, reduction, result, t, keep, away):
    dp_at, chan_at = device_at()
    for ref, core in ((keep, 0), (away, 1))[: plan.parts]:
        for j in range(reduction.blocks):
            if reduction.masks is None:
                owner_dp, owner = dp_at ^ core, j
            else:
                mask = reduction.masks[j]
                owner_dp, owner = dp_at ^ core ^ (mask // plan.n_chan), chan_at ^ (mask % plan.n_chan)
            first = owner * plan.out_own + (owner_dp & (reduction.parts - 1)) * reduction.part
            ref[j, t] = result[pl.ds(pl.multiple_of(first, 8), reduction.part)]


def weight_grad(plan, reduction, grad, even, odd, keep, away, result):
    left = split(grad.T)
    for a in range(3):
        for b in range(3):
            result[...] = dot3(left, read_tap(plan, even, odd, a, b), NN)
            place_rows(plan, reduction, result, 3 * a + b, keep, away)
    return left


def decoder_weight_kernel(plan, reduction, class_ref, gains, top_halo, decoder_norm, norm_rows, *refs):
    keep, away, result, even, odd = refs
    dp_at, chan_at = device_at()
    crop, strip = crop_strip(plan, dp_at, chan_at)
    wide = wide_rows(gains)
    inside = inside_mask(plan, class_ref, crop, strip, plan.n_out, True)
    fill_taps(plan, silu(decoder_norm[...] * wide[2] + norm_rows[2:3]) * inside, even, odd)
    weight_grad(plan, reduction, top_halo[SIDE : SIDE + plan.cells], even, odd, keep, away, result)


def middle_weight_kernel(
    plan, reduction, class_ref, gains, hidden_grad, middle_norm, entry_norm, shortcut, *refs
):
    shortcut_grad, keep, away, result, even, odd = refs
    dp_at, chan_at = device_at()
    crop, strip = crop_strip(plan, dp_at, chan_at)
    wide = wide_rows(gains)
    inside = inside_mask(plan, class_ref, crop, strip, plan.n_out, True)
    fill_taps(plan, silu(middle_norm[...] * wide[0] + wide[1]) * inside, even, odd)
    grad = hidden_grad[SIDE : SIDE + plan.cells]
    left = weight_grad(plan, reduction, grad, even, odd, keep, away, result)
    inside = inside[SIDE : SIDE + plan.cells, : plan.n_in]
    shortcut_in = (entry_norm[SIDE : SIDE + plan.cells] * gains[2:3] + gains[3:4]) * inside
    shortcut_grad[...] = dot3(split(grad), split(shortcut[...]), NN) * inside
    result[:, : plan.n_in] = dot3(left, split(shortcut_in), NN)
    result[:, plan.n_in :] = jnp.zeros((plan.n_out, plan.n_out - plan.n_in), f32)
    place_rows(plan, reduction, result, TAPS, keep, away)


def add_kernel(count, *refs):
    left, right, outs = refs[0], refs[1], refs[2:]
    size = left.shape[0] // count
    for k, out in enumerate(outs):
        out[...] = left[k * size : (k + 1) * size] + right[k * size : (k + 1) * size]


def total_kernel(*refs):
    out = refs[-1]
    total = refs[0][...]
    for ref in refs[1:-1]:
        total = total + ref[...]
    out[...] = total


def sum_blocks_kernel(blocks, out):
    total = blocks[0]
    for k in range(1, blocks.shape[0]):
        total = total + blocks[k]
    out[0] = total


def join_blocks_kernel(*refs):
    out, at = refs[-1], 0
    for ref in refs[:-1]:
        out[at : at + ref.shape[0]] = ref[...]
        at += ref.shape[0]


def pack_kernel(plan, parts, n_arrays, *refs):
    sources, tables, out, sems = refs[:n_arrays], refs[n_arrays:-2], refs[-2], refs[-1]
    dp_at, chan_at = device_at()
    part = plan.out_own // parts
    rows = pl.ds(pl.multiple_of((dp_at & (parts - 1)) * part, 8), part)
    copies, at = [], 0
    for k, source in enumerate(sources):
        if len(source.shape) == 3:
            copies.append(pltpu.make_async_copy(source.at[:, rows], out.at[at : at + TAPS], sems.at[k]))
            at += TAPS
        else:
            copies.append(pltpu.make_async_copy(source.at[rows], out.at[at], sems.at[k]))
            at += 1
        copies[-1].start()
    if tables:
        narrow, wide = tables[0][...], tables[1][...]
        narrow = jnp.concatenate([narrow, jnp.zeros((4, plan.n_in - plan.in_own), f32)], axis=1)
        narrow = jnp.concatenate([narrow, jnp.zeros((4, plan.n_in), f32)], axis=0)
        wide = jnp.concatenate([wide, jnp.zeros((5, plan.n_out - plan.out_own), f32)], axis=1)
        wide = jnp.concatenate([wide, jnp.zeros((3, plan.n_out), f32)], axis=0)
        narrow = pltpu.roll(narrow, chan_at * plan.in_own, 1)
        wide = pltpu.roll(wide, chan_at * plan.out_own, 1)
        pieces = [narrow[0:4]]
        for k in range(5):
            pieces += [wide[k : k + 1, : plan.n_in], wide[k : k + 1, plan.n_in :]]
        table = jnp.concatenate(pieces + [jnp.zeros((2, plan.n_in), f32)], axis=0)
        for k in range(16 // plan.part):
            out[at + k] = table[k * plan.part : (k + 1) * plan.part]
    wait_all(copies)


def held_sums(plan, recv):
    sums = []
    for which in range(plan.held):
        total = 0.0
        for strip in range(plan.strips):
            total = total + recv[which * plan.strips + gray(strip), :, plan.cells :]
        sums.append(total)
    return sums


def entry_sums_kernel(plan, recv, out):
    for which, total in enumerate(held_sums(plan, recv)):
        out[which] = jnp.concatenate([total, jnp.zeros((plan.in_own, 124), f32)], axis=1)


def own_gain_columns(plan, gains, row):
    _, chan_at = device_at()
    shape = (plan.in_own, plan.n_in)
    own = lax.broadcasted_iota(jnp.int32, shape, 0) + chan_at * plan.in_own
    pick = jnp.where(lax.broadcasted_iota(jnp.int32, shape, 1) == own, gains[row : row + 1], 0.0)
    return jnp.sum(pick, axis=1, keepdims=True)


def input_grad_kernel(plan, dp_masks, group_ref, class_ref, gains, recv, norm, scales, *refs):
    tiles, out = refs[:-1], refs[-1]
    dp_at, chan_at = device_at()
    entries, k = [], 0
    for ref in tiles:
        for block in range(ref.shape[0] // plan.held):
            for which in range(plan.held):
                entries.append(((dp_at ^ dp_masks[k]) * plan.held + which, ref, block * plan.held + which))
            k += 1
    gain_a, gain_b = own_gain_columns(plan, gains, 0), own_gain_columns(plan, gains, 2)
    for which in range(plan.held):
        crop = dp_at * plan.held + which
        count = group_cells(plan, group_ref, class_ref, crop)
        sums = 0.0
        for other, ref, at in entries:
            sums = sums + jnp.where(group_ref[other] == group_ref[crop], 1.0, 0.0).astype(f32) * ref[at]
        sums = sums / count
        shift = sums[:, 0:1] * gain_a + sums[:, 2:3] * gain_b
        slope = sums[:, 1:2] * gain_a + sums[:, 3:4] * gain_b
        pieces = [recv[which * plan.strips + gray(strip), :, : plan.cells] for strip in range(plan.strips)]
        joined = jnp.concatenate(pieces, axis=1)[:, : SIDE * SIDE]
        inside = crop_inside(plan, class_ref, dp_at, which, joined.shape)
        out[which] = scales[which][:, :1] * (joined - shift - norm[which] * slope) * inside


def join_kernel(plan, recv, out):
    for which in range(plan.held):
        pieces = [recv[which * plan.strips + gray(strip)] for strip in range(plan.strips)]
        out[which] = jnp.concatenate(pieces, axis=1)[:, : SIDE * SIDE]


def square_sum(values):
    values = values * values
    while values.ndim > 2:
        values = jnp.sum(values, axis=0)
    return jnp.sum(jnp.sum(values, axis=0, keepdims=True), axis=1, keepdims=True)


def wide_grads_kernel(plan, class_ref, pooled, decoder, middle, style_out, wide_out, squares, turned):
    dp_at, chan_at = device_at()
    vecs, grads, decoder_total, middle_total = [], [], 0.0, 0.0
    for other, mean in enumerate(crop_means(plan, class_ref, pooled)):
        row = unfold(mean)
        vecs.append(row * lax.rsqrt(jnp.sum(row * row, axis=1, keepdims=True) + style_eps))
        sums = crop_sums(plan, decoder, other)
        grads.append(unfold(sums[0:2]))
        decoder_total = decoder_total + sums
        middle_total = middle_total + crop_sums(plan, middle, other)
    blank = -len(vecs) % 8
    if blank:
        vecs.append(jnp.zeros((blank, plan.n_out), f32))
        grads.append(jnp.zeros((blank, plan.n_out), f32))
    vecs, grads = jnp.concatenate(vecs, axis=0), jnp.concatenate(grads, axis=0)
    turned[...] = grads.T
    own = turned[pl.ds(pl.multiple_of(chan_at * plan.out_own, 8), plan.out_own), :]
    style = lax.dot_general(own, vecs, NN, precision=highest, preferred_element_type=f32)
    style_out[...] = style

    first, second = unfold(middle_total[0:2]), unfold(middle_total[2:4])
    third, fourth = unfold(decoder_total[0:2]), unfold(decoder_total[2:4])
    wide = tile([second, first, fourth, third, third], plan.n_out)
    wide = pltpu.roll(wide, (plan.n_out - chan_at * plan.out_own) % plan.n_out, 1)[:5, : plan.out_own]
    wide_out[...] = wide
    squares[...] = jnp.broadcast_to((square_sum(style) + square_sum(wide)) * (1.0 / plan.n_dp), (8, 128))


def narrow_grads_kernel(plan, n_tiles, weights, early, *refs):
    tiles, sums, (narrow_out, squares) = refs[:n_tiles], refs[n_tiles:-2], refs[-2:]
    total = 0.0
    for ref in tiles:
        for at in range(ref.shape[0]):
            total = total + ref[at]
    lanes = jnp.concatenate([total, jnp.zeros((128 - plan.in_own, 128), f32)], axis=0).T
    narrow = jnp.concatenate([lanes[1:2], lanes[0:1], lanes[3:4], lanes[2:3]], axis=0)[:, : plan.in_own]
    narrow_out[...] = narrow
    share = square_sum(narrow) * (1.0 / plan.n_dp)
    for ref, weight in zip(sums, weights):
        share = share + square_sum(ref[0]) * weight
    total = (early[...] + share)[0:1]
    for device in range(squares.shape[0]):
        squares[device] = total


def update_kernel(plan, reductions, senders, counts, *refs):
    squares, refs = refs[: counts[0]], refs[counts[0] :]
    grads = []
    for count in counts[1:]:
        grads.append(refs[:count])
        refs = refs[count:]
    small, refs = refs[:3], refs[3:]
    held, refs = refs[:21], refs[21:]
    outs, norm_out, local, sems = refs[:21], refs[21], refs[22:-1], refs[-1]
    copies = []
    for k in range(21):
        copies.append(pltpu.make_async_copy(held[k], local[k], sems.at[k]))
        copies[-1].start()
    params, moments, seconds = local[:7], local[7:14], local[14:21]
    dp_at, chan_at = device_at()
    total = 0.0
    for device in range(squares[0].shape[0]):
        total = total + squares[0][device]
    norm = jnp.sqrt(total)
    norm_out[...] = norm[0:1, 0:1]
    factor = jnp.minimum(1.0, clip_bound / norm[0:1, 0:1])

    rates = (0.06, 0.04, 0.16, 0.04, 1.0, 0.4, 0.4)
    decays = (decay_rate, decay_rate, decay_rate, decay_rate, decay_rate, 0.0, 0.0)
    wait_all(copies)

    def update(which, at, gradient):
        new = adamw(
            params[which][at], gradient * factor, moments[which][at], seconds[which][at], rates[which], decays[which]
        )
        for ref, value in zip(outs[3 * which : 3 * which + 3], new):
            ref[at] = value

    for which, reduction, pieces, masks in zip((0, 1, 3), reductions, grads, senders):
        part = reduction.part
        for ref, mask in zip(pieces, masks):
            rows = pl.ds(pl.multiple_of(((dp_at ^ mask) & (reduction.parts - 1)) * part, 8), part)
            for t in range(TAPS):
                update(which, (t, rows, slice(None)), ref[0, t])
            if which == 1:
                update(2, (rows, slice(None)), ref[0, TAPS, :, : plan.n_in])
    for which, ref in zip((4, 5, 6), small):
        update(which, (slice(None), slice(None)), ref[...])


class Slot:
    def __init__(self, store, at, shape):
        self.store, self.at, self.shape, self.size = store, at, shape, functools.reduce(lambda x, y: x * y, shape)

    def view(self, ref):
        return ref.at[(self.at,) + tuple(slice(0, n) for n in self.shape)]


class Fetched:
    def __init__(self, source, local, sem):
        self.copy, self.local, self.waits = pltpu.make_async_copy(source, local, sem), local, True
        self.shape = local.shape
        self.copy.start()

    def __getitem__(self, at):
        self.wait()
        return self.local[at]

    def wait(self):
        if self.waits:
            self.copy.wait()
        self.waits = False


class Saved:
    def __init__(self, target, local, sem):
        self.target, self.local, self.sem, self.copy = target, local, sem, None

    def __setitem__(self, at, value):
        self.local[...] = value
        self.take(self.local)

    def take(self, ref):
        self.copy = pltpu.make_async_copy(ref, self.target, self.sem)
        self.copy.start()

    def wait(self):
        self.copy.wait()


class Chain:
    def __init__(self, stores):
        self.last, self.cost = None, COST
        self.shapes, self.stores, self.used = stores, {}, {name: 0 for name in stores}

    def slot(self, shape, store="maps"):
        self.used[store] += 1
        return Slot(store, self.used[store] - 1, shape)

    def run(
        self, name, kernel, smem, arrays, out_shapes, scratch=(), flops=0, far=(), more=(), limit=None, passed=None,
        cost=None,
    ):
        cost = self.cost if cost is None else cost
        wanted = [*smem, *arrays, *far, *more]
        spaces = [SMEM] * len(smem) + [VMEM] * len(arrays)
        spaces += [pl.BlockSpec(memory_space=pl.ANY)] * len(far) + [VMEM] * len(more)
        operands = [a for a in wanted if not isinstance(a, Slot)]
        specs = [space for a, space in zip(wanted, spaces) if not isinstance(a, Slot)]
        loads = [a for a in wanted if isinstance(a, Slot)]
        saves = [shape for shape in out_shapes if isinstance(shape, Slot)]
        plain = [shape for shape in out_shapes if not isinstance(shape, Slot)]
        sizes = [functools.reduce(lambda x, y: x * y, shape) for shape in plain]
        small = bool(sizes) and min(sizes) <= 8 * 1024
        shapes = [jax.ShapeDtypeStruct(shape, f32) for shape in plain + ([] if small else [(8, 128)])]
        out_specs, aliases = [VMEM] * len(shapes), {}
        anywhere = pl.BlockSpec(memory_space=pl.ANY)
        rest = [] if self.last is None else [self.last]
        touched = sorted({slot.store for slot in loads + saves})
        for store in touched:
            if store in self.stores:
                rest.append(self.stores[store])
                aliases[len(operands) + len(rest) - 1] = len(shapes)
            shapes.append(jax.ShapeDtypeStruct(self.shapes[store], f32))
            out_specs.append(anywhere)
        if passed is not None:
            rest.append(passed)
            aliases[len(operands) + len(rest) - 1] = len(shapes)
            shapes.append(jax.ShapeDtypeStruct(passed.shape, f32))
            out_specs.append(anywhere)
        moved = 4 * sum(int(a.size) for a in wanted) + 4 * sum(sizes) + 4 * sum(slot.size for slot in saves)
        local = [pltpu.VMEM(slot.shape, f32) for slot in loads + saves]
        if local:
            local.append(pltpu.SemaphoreType.DMA((len(local),)))
        n_plain = len(plain)

        def called(*refs):
            ins, refs = list(refs[: len(operands)]), refs[len(operands) + len(rest) :]
            outs, own, refs = refs[:n_plain], refs[n_plain : len(shapes)], refs[len(shapes) :]
            if not small:
                own[0][...] = jnp.zeros((8, 128), f32)
                own = own[1:]
            stores = dict(zip(touched, own))
            buffers, refs = refs[: len(local)], refs[len(local) :]
            opened = []
            for at, slot in enumerate(loads + saves):
                kind = Fetched if at < len(loads) else Saved
                opened.append(kind(slot.view(stores[slot.store]), buffers[at], buffers[-1].at[at]))
            fetched, saved = iter(opened[: len(loads)]), iter(opened[len(loads) :])
            ins, outs = iter(ins), iter(outs)
            taken = [next(fetched) if isinstance(a, Slot) else next(ins) for a in wanted]
            given = [next(saved) if isinstance(a, Slot) else next(outs) for a in out_shapes]
            kernel(*taken, *given, *refs)
            for one in opened:
                one.wait()

        outs = list(pl.pallas_call(
            called,
            out_shape=shapes,
            in_specs=specs + [anywhere] * len(rest),
            out_specs=out_specs,
            input_output_aliases=aliases,
            scratch_shapes=local + list(scratch),
            cost_estimate=pl.CostEstimate(flops=cost * flops, bytes_accessed=cost * moved, transcendentals=0),
            compiler_params=pltpu.CompilerParams(vmem_limit_bytes=limit or VMEM_LIMIT),
            name=name,
        )(*operands, *rest))
        self.last = outs[sizes.index(min(sizes))] if small else outs[n_plain]
        first = n_plain + (0 if small else 1)
        for k, store in enumerate(touched):
            self.stores[store] = outs[first + k]
        results = iter(outs[:n_plain])
        given = [a if isinstance(a, Slot) else next(results) for a in out_shapes]
        return given if passed is None else given + [outs[-1]]


def adamw(weight, gradient, moment, square, rate, decay):
    first_new = beta_one * moment + (1.0 - beta_one) * gradient
    second_new = beta_two * square + (1.0 - beta_two) * gradient * gradient
    corrected_first = first_new / (1.0 - beta_one**STEP)
    corrected_second = second_new / (1.0 - beta_two**STEP)
    updated = weight - rate * (
        corrected_first / (jnp.sqrt(corrected_second) + adam_eps) + decay * weight
    )
    return (updated, first_new, second_new)


def make_body(mesh):
    def body(
        crop_maps, out_cotangent, norm_group, scale_class,
        entry_conv, middle_conv, shortcut_map, decoder_conv, style_map, narrow_gain_table, wide_gain_table,
        entry_moment, middle_moment, shortcut_moment, decoder_moment, style_moment, narrow_moment, wide_moment,
        entry_square, middle_square, shortcut_square, decoder_square, style_square, narrow_square, wide_square,
    ):
        plan = Plan(mesh, crop_maps.shape, out_cotangent.shape)
        n_in, n_out, n_chan = plan.n_in, plan.n_out, plan.n_chan
        cells, cells_halo = plan.cells, plan.cells_halo
        ids = (norm_group, scale_class)
        weight_shape = (n_chan, plan.parts, TAPS, plan.part, n_out)
        chain = Chain({"maps": (STORED_MAPS, cells_halo, n_out), "weights": (STORED_WEIGHTS,) + weight_shape})
        run, slot = chain.run, chain.slot

        def dp_swap(block, mask):
            return lax.ppermute(block, "dp", [(i, i ^ mask) for i in range(plan.n_dp)])

        def gather_dp(name, block):
            tiles, masks = [block], [0]
            for stage in pair_bits(plan.dp_bits):
                joined = tiles[0] if len(tiles) == 1 else jnp.concatenate(tiles, axis=0)
                with jax.named_scope(name):
                    tiles = [joined] + [dp_swap(joined, mask) for mask in stage]
                masks = masks + [held ^ mask for mask in stage for held in masks]
            return tiles, masks

        def exchange(name, messages):
            everyone, edge_a, edge_b = messages
            with jax.named_scope(name):
                rows = lax.all_to_all(everyone, BOTH, 0, 0)
            if plan.quick:
                with jax.named_scope(name + "_edges"):
                    return rows, swap(edge_a, plan.strip_bits[0], plan), swap(edge_b, plan.strip_bits[1], plan)
            up, down = [], []
            for crop in range(plan.n_crops):
                devices = plan.devices_of(crop)
                down += list(zip(devices[:-1], devices[1:]))
                up += list(zip(devices[1:], devices[:-1]))
            with jax.named_scope(name + "_edges"):
                return rows, lax.ppermute(edge_a, BOTH, down), lax.ppermute(edge_b, BOTH, up)

        by_tap = lambda weight: jnp.transpose(weight, (1, 0, 2))
        n_tables = 16 // plan.part
        stages = pair_bits(plan.chan_bits[:0:-1]) + [[plan.chan_bits[0]]]

        def pack(name, parts, arrays, tables=()):
            taps = sum(TAPS if a.ndim == 3 else 1 for a in arrays) + (n_tables if tables else 0)
            return run(
                name + "_pack", functools.partial(pack_kernel, plan, parts, len(arrays)), (), (),
                [(taps, plan.out_own // parts, arrays[0].shape[-1])], [pltpu.SemaphoreType.DMA((len(arrays),))],
                far=arrays, more=tables,
            )[0]

        class Gathering:
            def __init__(self, name, parts, packed):
                self.name, self.parts = name, parts
                self.block, self.masks, self.left = packed[None], [0], list(stages)
                self.send()

            def send(self):
                stage = self.left.pop(0)
                with jax.named_scope(self.name):
                    self.arrived = [swap(self.block, mask, plan) for mask in stage]
                self.masks = self.masks + [held ^ mask for mask in stage for held in self.masks]

            def join(self):
                joined = [self.block] + self.arrived
                shape = (sum(x.shape[0] for x in joined),) + self.block.shape[1:]
                self.block = run(self.name + "_join", join_blocks_kernel, (), joined, [shape])[0]

            def along_y(self):
                while len(self.left) > 1:
                    self.join()
                    self.send()
                self.join()
                self.send()

            def finish(self, joined):
                if joined:
                    self.join()
                    arrays, senders = [self.block], [(0, self.masks)]
                else:
                    half = len(self.masks) // 2
                    arrays = [self.block] + self.arrived
                    senders = [(0, self.masks[:half]), (0, self.masks[half:])]
                for bit in plan.dp_bits[::-1]:
                    if bit < self.parts:
                        with jax.named_scope(self.name + "_dp"):
                            arrays = arrays + [swap(block, bit * n_chan, plan) for block in arrays]
                        senders = senders + [(dp_mask ^ bit, chans) for dp_mask, chans in senders]
                return Packet(arrays, senders, self.parts)

        packed = pack("wide_weights", plan.parts, (by_tap(middle_conv), by_tap(decoder_conv), style_map))
        with jax.named_scope("wide_weights"):
            gathered = lax.all_gather(packed, "chan")

        maps_shape = crop_maps.shape
        stats = run(
            "entry_stats", functools.partial(stats_kernel, plan), (scale_class,), (crop_maps,),
            [(2, plan.held, plan.in_own, 128)],
        )[0]
        dp_tiles, dp_masks = gather_dp("entry_stats", stats)
        entry_gathering = Gathering(
            "entry_weights", plan.parts,
            pack("entry_weights", plan.parts, (by_tap(entry_conv), shortcut_map), (narrow_gain_table, wide_gain_table)),
        )
        norm_held, scales, send = run(
            "entry_norm", functools.partial(norm_kernel, plan, dp_masks), ids, (crop_maps, *dp_tiles),
            [maps_shape, (plan.held, plan.in_own, 128), (n_chan, plan.in_own, cells_halo)],
        )
        with jax.named_scope("maps"):
            recv = lax.all_to_all(send, "chan", 0, 0).reshape(n_in, cells_halo)
        entry_gathering.along_y()
        narrow = entry_gathering.finish(False)
        top_send = run(
            "pack_top", functools.partial(top_kernel, plan), (scale_class,), (out_cotangent,),
            [(n_chan, plan.out_own, cells_halo)],
        )[0]

        message_shapes = [(plan.n_all, 4, n_out // 2), (SIDE, n_out), (SIDE, n_out)]
        wide_taps, narrow_taps = tap_scratch(plan, n_out), tap_scratch(plan, n_in)
        flat_narrow = pltpu.VMEM((n_out, n_in), f32)
        entry_weight, entry_rest = narrow.scratch(plan, TAPS, n_in), narrow.scratch(plan, 1 + n_tables, n_in)
        flat_wide = pltpu.VMEM((n_out, n_out), f32)
        wide_flops = 2 * 3 * TAPS * cells * n_out * n_out
        narrow_flops = 2 * 3 * TAPS * cells * n_out * n_in

        entry_norm, gains, first_out, shortcut, entry_kept, *messages = run(
            "first_conv", functools.partial(first_kernel, plan, narrow), (scale_class,), (recv,),
            [slot((cells_halo, n_in)), slot((16, n_in)), slot((cells, n_out)), slot((n_out, n_in)),
             slot(weight_shape[:-1] + (n_in,), "weights")] + message_shapes,
            [entry_weight[0], entry_rest[0], entry_weight[1], entry_rest[1]] + narrow_taps, narrow_flops,
            far=narrow.arrays,
        )
        first_stats, edge_a, edge_b = exchange("first_stats", messages)
        top_send = run("top_gate", gate_kernel, (), (first_stats, edge_a, edge_b), [(8, 128)], passed=top_send)[1]
        with jax.named_scope("top"):
            top_recv = lax.all_to_all(top_send, "chan", 0, 0).reshape(n_out, cells_halo)
        gathered = run("wide_weights_gate", gate_kernel, (), (), [(8, 128)], passed=gathered)[1]
        arrays, senders = [gathered], [(0, None)]
        if plan.parts > 1:
            with jax.named_scope("wide_weights_core"):
                arrays, senders = arrays + [swap(gathered, plan.core_mask, plan)], senders + [(1, None)]
        middle, decoder = Packet(arrays, senders, plan.parts), Packet(arrays, senders, plan.parts, TAPS)
        middle_weight = middle.scratch(plan, TAPS, n_out)
        decoder_weight, style_flat = decoder.scratch(plan, TAPS, n_out), decoder.scratch(plan, 1, n_out)

        middle_norm, middle_rows, hidden, middle_kept, *messages = run(
            "second_conv", functools.partial(hidden_kernel, plan, middle), ids,
            (gains, first_out, edge_a, edge_b, entry_norm, first_stats, shortcut),
            [slot((cells_halo, n_out)), slot((8, n_out)), slot((cells, n_out)), slot(weight_shape, "weights")]
            + message_shapes,
            middle_weight + wide_taps, wide_flops, far=middle.arrays,
        )
        hidden_stats, edge_a, edge_b = exchange("hidden_stats", messages)

        top_halo, top_back, style, decoder_kept = run(
            "top_back", functools.partial(top_back_kernel, plan, decoder), (), (top_recv,),
            [slot((cells_halo, n_out)), slot((cells, n_out)), slot((n_out, n_out)), slot(weight_shape, "weights")],
            [decoder_weight[0], style_flat[0], decoder_weight[1], style_flat[1]] + wide_taps, wide_flops,
            far=decoder.arrays, cost=HIDE,
        )

        decoder_norm, decoder_rows, decoder_pre_grad, *messages = run(
            "decoder_norm", functools.partial(decoder_kernel, plan), ids,
            (gains, hidden, edge_a, edge_b, top_back, hidden_stats, style),
            [slot((cells_halo, n_out)), slot((8, n_out)), slot((cells, n_out))] + message_shapes,
        )
        decoder_sums, edge_a, edge_b = exchange("decoder_sums", messages)

        def add(name, left, right, count):
            shape = (left.shape[0] // count,) + left.shape[1:]
            return run(name + "_add", functools.partial(add_kernel, count), (), (left, right), [shape] * count)

        def sum_cores(name, halves, count):
            keep, away = halves
            if plan.parts == 1:
                return [keep[k * keep.shape[0] // count : (k + 1) * keep.shape[0] // count] for k in range(count)]
            with jax.named_scope(name + "_core"):
                arrived = swap(away, plan.core_mask, plan)
            return add(name, keep, arrived, count)

        def sum_far(name, total, reduction):
            for bit in plan.dp_bits:
                if bit >= reduction.parts:
                    with jax.named_scope(name + "_far"):
                        arrived = swap(total, bit * n_chan, plan)
                    total = run(name + "_total", total_kernel, (), (total, arrived), [total.shape])[0]
            return total

        def all_parts(name, total, reduction):
            masks = list(range(reduction.parts))
            with jax.named_scope(name + "_back"):
                return [total] + [swap(total, mask * n_chan, plan) for mask in masks[1:]], masks

        def halve(name, pair, bit, last):
            with jax.named_scope(name + "_half"):
                arrived = swap(pair[1], bit, plan)
            return add(name, pair[0], arrived, pair[0].shape[0] if last else 2)

        def collect(name, blocks, reduction):
            with jax.named_scope(name + "_last"):
                arrived = [swap(b, mask, plan) for b, mask in zip(blocks[1:], reduction.last[1:])]
            return run(name + "_total", total_kernel, (), (blocks[0], *arrived), [blocks[0].shape])[0]

        decoder_plan = Reduction(plan, TAPS, plan.parts)
        cross = [2 * n_chan] if plan.wide_parts > 2 else []
        middle_plan = Reduction(plan, TAPS + 1, plan.wide_parts, cross + plan.chan_bits[:1])
        entry_plan = Reduction(plan, TAPS, plan.parts, plan.chan_bits[:1])

        decoder_halves = run(
            "decoder_wgrad", functools.partial(decoder_weight_kernel, plan, decoder_plan), (scale_class,),
            (gains, top_halo, decoder_norm, decoder_rows), [decoder_plan.shape(n_out)] * 2,
            [flat_wide] + wide_taps, wide_flops, cost=HIDE,
        )
        out_send = run(
            "decoder_conv", functools.partial(out_kernel, plan), (scale_class,),
            (gains, hidden, decoder_norm, decoder_rows, decoder_kept),
            [(n_chan, plan.out_own, cells)], wide_taps, wide_flops, cost=HIDE,
        )[0]

        hidden_grad, middle_pre_grad, *messages = run(
            "second_back", functools.partial(hidden_back_kernel, plan), ids,
            (gains, decoder_pre_grad, edge_a, edge_b, decoder_norm, decoder_rows, top_halo, middle_norm,
             decoder_sums, style, middle_kept),
            [slot((cells_halo, n_out)), slot((cells, n_out))] + message_shapes,
            wide_taps, wide_flops,
        )
        middle_sums, edge_a, edge_b = exchange("middle_sums", messages)
        chain.cost = MIDDLE
        decoder_half = sum_cores("decoder_grads", decoder_halves, 1)[0]
        with jax.named_scope("decoder_grads_scatter"):
            decoder_grads = lax.psum_scatter(decoder_half, "chan", scatter_dimension=0, tiled=True)
        shortcut_grad, *middle_halves = run(
            "middle_wgrad", functools.partial(middle_weight_kernel, plan, middle_plan), (scale_class,),
            (gains, hidden_grad, middle_norm, entry_norm, shortcut),
            [slot((cells, n_in))] + [middle_plan.shape(n_out)] * 2,
            [flat_wide] + wide_taps, wide_flops, cost=MIDDLE,
        )
        out_send = run("block_gate", gate_kernel, (), (middle_sums, edge_a, edge_b), [(8, 128)], passed=out_send)[1]
        with jax.named_scope("block_out"):
            out_recv = lax.all_to_all(out_send, "chan", 0, 0)

        chain.cost = TAIL
        first_grad, *halves = run(
            "first_grad", functools.partial(first_grad_kernel, plan, entry_plan), ids,
            (gains, middle_pre_grad, edge_a, edge_b, middle_norm, middle_rows, entry_norm, middle_sums),
            [slot((cells_halo, n_out))] + [entry_plan.shape(n_in)] * 2, [flat_narrow] + narrow_taps, narrow_flops,
        )

        entry_pair = sum_cores("entry_grads", halves, 2)
        middle_pair = sum_cores("middle_grads", middle_halves, 2)
        block_out = run(
            "block_out", functools.partial(join_kernel, plan), (), (out_recv,), [out_cotangent.shape], cost=HIDE
        )[0]
        entry_blocks = halve("entry_grads", entry_pair, plan.chan_bits[0], True)
        send = run(
            "first_back", functools.partial(first_back_kernel, plan), (scale_class,),
            (gains, first_grad, entry_norm, shortcut_grad, entry_kept),
            [(n_chan, plan.in_own, cells + 4)], wide_taps, narrow_flops,
        )[0]
        with jax.named_scope("input_grad"):
            recv = lax.all_to_all(send, "chan", 0, 0)
        for k, bit in enumerate(middle_plan.halving[:-1]):
            middle_pair = halve("middle_grads", middle_pair, bit, False)
        style_sum, wide_sum, early_share = run(
            "wide_grads", functools.partial(wide_grads_kernel, plan), (scale_class,),
            (hidden_stats, decoder_sums, middle_sums), [(plan.out_own, n_out), (5, plan.out_own), (8, 128)],
            [pltpu.VMEM((n_out, -(-plan.n_crops // 8) * 8), f32)],
        )
        entry_sums = run(
            "entry_sums", functools.partial(entry_sums_kernel, plan), (), (recv,), [(plan.held, plan.in_own, 128)]
        )[0]
        entry_tiles, entry_masks = gather_dp("entry_sums", entry_sums)
        entry_total = collect("entry_grads", entry_blocks, entry_plan)
        middle_blocks = halve("middle_grads", middle_pair, middle_plan.halving[-1], True)
        entry_total = sum_far("entry_grads", entry_total, entry_plan)
        input_grad = run(
            "input_grad", functools.partial(input_grad_kernel, plan, entry_masks), ids,
            (gains, recv, norm_held, scales, *entry_tiles), [maps_shape],
        )[0]
        middle_total = collect("middle_grads", middle_blocks, middle_plan)
        middle_total = sum_far("middle_grads", middle_total, middle_plan)
        decoder_total = sum_far("decoder_grads", decoder_grads, decoder_plan)
        totals, plans = [entry_total, middle_total, decoder_total], [entry_plan, middle_plan, decoder_plan]
        names = ("entry_grads", "middle_grads", "decoder_grads")
        parted = [all_parts(name, total, held) for name, total, held in zip(names, totals, plans)]
        pieces, senders = [p for p, _ in parted], [m for _, m in parted]
        narrow_sum, squares = run(
            "narrow_grads", functools.partial(narrow_grads_kernel, plan, len(entry_tiles), [p.parts / plan.n_dp for p in plans]), (),
            (early_share, *entry_tiles, *totals), [(4, plan.in_own), (plan.n_all, 1, 128)],
        )
        with jax.named_scope("norm"):
            tiles = [lax.all_to_all(squares, BOTH, 0, 0)]
        params = (entry_conv, middle_conv, shortcut_map, decoder_conv, style_map, narrow_gain_table, wide_gain_table)
        moments = (
            entry_moment, middle_moment, shortcut_moment, decoder_moment, style_moment, narrow_moment, wide_moment,
        )
        seconds = (
            entry_square, middle_square, shortcut_square, decoder_square, style_square, narrow_square, wide_square,
        )
        turned = [by_tap(a) if a.ndim == 3 else a for a in params + moments + seconds]
        counts = [len(tiles)] + [len(p) for p in pieces]
        *updated, norm = run(
            "update", functools.partial(update_kernel, plan, plans, senders, counts), (),
            (*tiles, *[p for held in pieces for p in held], style_sum, narrow_sum, wide_sum),
            [p.shape for p in turned[:7] for _ in range(3)] + [(1, 1)],
            [pltpu.VMEM(p.shape, f32) for p in turned] + [pltpu.SemaphoreType.DMA((21,))],
            far=turned, limit=60 * 2**20,
        )
        updated = [by_tap(a) if a.ndim == 3 else a for a in updated]
        return (block_out, input_grad, *updated, norm.reshape(()))

    return body


def solution(mesh):
    maps, whole = P("dp", "chan", None), P()
    conv_spec, flat_spec, table_spec = P("chan", None, None), P("chan", None), P(None, "chan")
    params = (conv_spec, conv_spec, flat_spec, conv_spec, flat_spec, table_spec, table_spec)
    updated = tuple(spec for spec in params for _ in range(3))
    return jax.shard_map(
        make_body(mesh),
        mesh=mesh,
        in_specs=(maps, maps, whole, whole) + params * 3,
        out_specs=(maps, maps) + updated + (whole,),
        check_vma=False,
    )
```
